256 devices in a mesh: dp: 4 (over y), expert: 64 (over x, z, core).
Axes of the slice: x: 4, y: 4, z: 8, core: 2. Of those that a mesh axis runs over, the one named last changes fastest.
Arguments:
- tokens: bfloat16 [32768, 2048], P(('dp', 'expert')), parts along dimension 0, may hold values from -6 to 6
- cotangent: bfloat16 [32768, 2048], P(('dp', 'expert')), parts along dimension 0, may hold values from -6 to 6
- routes: int32 [32768, 8], P(('dp', 'expert')), parts along dimension 0, may hold values from 0 to 63, all different within a row; in each aligned block of 128 rows (0 to 127, 128 to 255, ...) at most 18 rows name the same one
- route_weight: float32 [32768, 8], P(('dp', 'expert')), parts along dimension 0, may hold values from 0.1 to 1
- example_ids: int32 [32768], P(('dp', 'expert')), parts along dimension 0, may hold values from 0 to 1
- w_gate: bfloat16 [64, 2048, 768], P('expert'), may hold values from -0.125 to 0.125
- w_up: bfloat16 [64, 2048, 768], P('expert'), may hold values from -0.125 to 0.125
- w_down: bfloat16 [64, 768, 2048], P('expert'), may hold values from -0.21875 to 0.21875
- proj_model: bfloat16 [64, 2048], replicated, may hold values from -0.125 to 0.125
- proj_hidden: bfloat16 [64, 768], replicated, may hold values from -0.21875 to 0.21875
Outputs:
- proj_grads: bfloat16 [512, 64, 2, 4096], P(('dp', 'expert')), parts along dimension 0
The draws below stay inside these ranges and needn't reach their ends.
There are 4 independent parts, one for each index of `dp`. The reference program is written for one: setup_inputs(seed, part) draws one part's arguments, and reference() takes and returns one part's arrays. A program takes and returns all parts, laid end to end along the dimension named above; an argument that names none is the same for every part. Nothing has to cross between parts.
Inputs may be any that keep to these rules, and one draw needn't show every extreme that they name: `routes`: each token names 8 different experts; among the rows of one device at most 18 name any one expert.
All inputs are finite; a program needn't handle non-finite values.
Results may differ from the reference program's by a relative error of at most 0.007.
Values may be sent and summed in bfloat16 or wider, within the bound.
No kernel may reach another device: no remote copies, remote signals or barrier semaphores. Data moves between devices by JAX's collectives and lax.ppermute only.
A program may use at most 128 MiB of HBM per device.

```python
import math
import jax
import jax.numpy as jnp
import numpy as np
from jax import lax

D = 2048
FF = 768
TOP = 8
R = 64
TOK_DEV = 128
EX_DEV = 2
EXPERTS = 64
CAP = 18
TOKENS = 8192
EXAMPLES = 128
N_EXPERT = 64


def with_ends(array, own_key, smallest, largest):
    spot = [jax.random.randint(jax.random.fold_in(own_key, axis), (), 0, length) for axis, length in enumerate(array.shape)]
    widest = array.shape.index(max(array.shape))
    neighbour = spot[:widest] + [(spot[widest] + 1) % array.shape[widest]] + spot[widest + 1:]
    return array.at[tuple(spot)].set(smallest).at[tuple(neighbour)].set(largest)


def levels(own_key, shape, shards, least, high):
    gain, own = 1.0, jax.random.fold_in(own_key, 6)
    for position, shards_of in shards:
        heights = jnp.exp(jax.random.uniform(jax.random.fold_in(own, position), (shards_of,), jnp.float32, least / len(shards), high / len(shards)))
        gain = gain * jnp.repeat(heights, shape[position] // shards_of).reshape([-1 if axis == position else 1 for axis in range(len(shape))])
    return gain


def shared_out(rng, own, number, rows, count, top, limit, slope):
    sequence = jax.random.permutation(rng, count)
    heavy_load, common = portions_of(count, rows * top, limit, slope, True), portions_of(count, rows * top, limit, slope, False)
    places = jnp.arange(count)

    def named(sizes, rotation):
        used = int((sizes > 0).sum())
        fixed = max(1, used // 4)
        shifted = fixed + (places - fixed + rotation * (used - fixed)) % max(1, count - fixed)
        return jnp.zeros((count,), jnp.int32).at[sequence[jnp.where(places < fixed, places, shifted)]].set(jnp.asarray(sizes, jnp.int32))

    sizes = jnp.where(number % 4 == 0, named(heavy_load, number // 4), named(common, number - number // 4 - 1))
    mixed = jax.random.permutation(jax.random.fold_in(own, 3), count)
    giver, taker = mixed[0:count // 2 * 2:2], mixed[1:count // 2 * 2:2]
    slack = jnp.minimum(sizes[giver] - 1, limit - sizes[taker]) // 2
    slack = jnp.where((giver == sequence[0]) | (taker == sequence[0]) | (sizes[taker] == 0), 0, jnp.maximum(slack, 0))
    shifted = jax.random.randint(jax.random.fold_in(own, 4), (count // 2,), 0, 1 << 20) % (slack + 1)
    sizes = sizes.at[giver].add(-shifted).at[taker].add(shifted)
    labels = jnp.searchsorted(jnp.cumsum(sizes), jnp.arange(rows * top), side="right").astype(jnp.int32)
    grid = labels.reshape(top, rows).T
    grid = grid[jax.random.permutation(jax.random.fold_in(own, 1), rows)]
    rotation = jax.random.randint(jax.random.fold_in(own, 2), (rows, 1), 0, top)
    return jnp.take_along_axis(grid, (jnp.arange(top)[None, :] + rotation) % top, axis=1)


def portions_of(count, total, bound, skew, full):
    weights = [(1 << 20) // math.isqrt(standing ** skew) + 1 for standing in range(1, count + 1)]
    largest = bound if full else min(bound, max(-(-total // count), total * weights[0] // sum(weights)))
    least = 1 if total - largest >= count - 1 else 0
    holding, spare = [largest] + [least] * (count - 1), total - largest - least * (count - 1)
    while spare > 0:
        free = [i for i in range(1, count) if holding[i] < largest] or [i for i in range(1, count) if holding[i] < bound]
        mass, budget = sum([weights[i] for i in free]), spare
        for i in free:
            addition = min(bound - holding[i], max(1, budget * weights[i] // mass), spare)
            holding[i] = holding[i] + addition
            spare = spare - addition
    return np.array(holding)


def scatter_about(own_key, dims, scale, bound, split=(), kind=jnp.bfloat16):
    result = scale * jax.random.normal(own_key, dims, jnp.float32)
    if split:
        result = result * levels(own_key, dims, split, -0.22, 0.18)
    return jnp.clip(result, -bound, bound).astype(kind)


def setup_inputs(seed: int = 0, part: int = 0) -> dict:
    keys = jax.random.split(jax.random.key(seed), 11)
    part_keys = jax.random.split(jax.random.fold_in(keys[10], part), 11)
    tokens = scatter_about(part_keys[0], (TOKENS, D), 1.0, 6.0, ((0, 64),))
    cotangent = scatter_about(part_keys[1], (TOKENS, D), 1.0, 6.0, ((0, 64),))
    routes_keys = jax.random.split(jax.random.fold_in(part_keys[2], 1), TOKENS // TOK_DEV)
    routes_turns = jax.random.permutation(jax.random.fold_in(part_keys[2], 3), TOKENS // TOK_DEV)
    routes = jax.vmap(lambda own, number: shared_out(jax.random.fold_in(part_keys[2], 2), own, number, TOK_DEV, EXPERTS, TOP, CAP, 2))(routes_keys, routes_turns).reshape((TOKENS, TOP))
    route_weight = jnp.clip(0.1 + 0.9 * jax.random.uniform(part_keys[3], (TOKENS, TOP), jnp.float32) ** levels(part_keys[3], (TOKENS, TOP), ((0, 64),), -0.2, 0.2), 0.1, 1.0)
    example_ids = with_ends(jax.random.randint(part_keys[4], (TOKENS,), 0, EX_DEV), jax.random.fold_in(part_keys[4], 1), 0, EX_DEV - 1).astype(jnp.int32)
    w_gate = scatter_about(keys[5], (EXPERTS, D, FF), D ** -0.5, 0.125, ((0, 64),))
    w_up = scatter_about(keys[6], (EXPERTS, D, FF), D ** -0.5, 0.125, ((0, 64),))
    w_down = scatter_about(keys[7], (EXPERTS, FF, D), FF ** -0.5, 0.21875, ((0, 64),))
    proj_model = scatter_about(keys[8], (R, D), D ** -0.5, 0.125)
    proj_hidden = scatter_about(keys[9], (R, FF), FF ** -0.5, 0.21875)
    return {"tokens": tokens, "cotangent": cotangent, "routes": routes, "route_weight": route_weight, "example_ids": example_ids, "w_gate": w_gate, "w_up": w_up, "w_down": w_down, "proj_model": proj_model, "proj_hidden": proj_hidden}


def project(rows, proj):
    return jnp.dot(rows, proj.T, preferred_element_type=jnp.float32).astype(jnp.bfloat16)


def reference(tokens, cotangent, routes, route_weight, example_ids, w_gate, w_up, w_down, proj_model, proj_hidden):
    count = TOKENS * TOP
    width = N_EXPERT * CAP
    flat_e = routes.reshape(-1).astype(jnp.int32)
    onehot = (flat_e[:, None] == jnp.arange(EXPERTS, dtype=jnp.int32)[None, :]).astype(jnp.int32)
    rank = jnp.sum((jnp.cumsum(onehot, axis=0) - onehot) * onehot, axis=1).astype(jnp.int32)
    table = jnp.full((EXPERTS * width,), count, jnp.int32)
    table = table.at[flat_e * width + rank].set(jnp.arange(count, dtype=jnp.int32)).reshape(EXPERTS, width)
    in_model_tok = project(tokens, proj_model)
    example_global = ((jnp.arange(TOKENS, dtype=jnp.int32) // TOK_DEV) * EX_DEV + example_ids).astype(jnp.int32)
    flat_weight = route_weight.reshape(-1)

    def one_expert(inputs):
        gate_w, up_w, down_w, index = inputs
        valid = index < count
        safe = jnp.minimum(index, count - 1)
        tok = safe // TOP
        xrows = jnp.where(valid[:, None], tokens[tok], jnp.zeros((), tokens.dtype))
        wslot = jnp.where(valid, flat_weight[safe], jnp.zeros((), flat_weight.dtype))
        dgrows = (wslot[:, None] * cotangent[tok].astype(jnp.float32)).astype(jnp.bfloat16)
        gate = jnp.dot(xrows, gate_w, preferred_element_type=jnp.float32)
        upval = jnp.dot(xrows, up_w, preferred_element_type=jnp.float32)
        sig = jax.nn.sigmoid(gate)
        hidden = (gate * sig * upval).astype(jnp.bfloat16)
        back = jnp.dot(dgrows, down_w.T, preferred_element_type=jnp.float32)
        delta = (back * upval * sig * (1.0 + gate * (1.0 - sig))).astype(jnp.bfloat16)
        in_hidden = project(hidden, proj_hidden).astype(jnp.float32)
        out_hidden = project(delta, proj_hidden).astype(jnp.float32)
        in_model = jnp.where(valid[:, None], in_model_tok[tok], jnp.zeros((), in_model_tok.dtype)).astype(jnp.float32)
        out_model = project(dgrows, proj_model).astype(jnp.float32)
        seg = jnp.where(valid, example_global[tok], EXAMPLES).astype(jnp.int32)
        gate_outer = (in_model[:, :, None] * out_hidden[:, None, :]).reshape(width, R * R)
        down_outer = (in_hidden[:, :, None] * out_model[:, None, :]).reshape(width, R * R)
        gate_sum = jax.ops.segment_sum(gate_outer, seg, num_segments=EXAMPLES)
        down_sum = jax.ops.segment_sum(down_outer, seg, num_segments=EXAMPLES)
        return jnp.stack([gate_sum, down_sum], axis=1)

    sums = lax.map(one_expert, (w_gate, w_up, w_down, table))
    return jnp.transpose(sums, (1, 0, 2, 3)).astype(jnp.bfloat16)
```

```python
import jax
import jax.numpy as jnp
from jax import lax
from jax.experimental import pallas as pl
from jax.experimental.pallas import tpu as pltpu
from jax.sharding import Mesh
from jax.sharding import PartitionSpec as P

NX, NZ, NC = 4, 8, 2
NJ = NX * NC
CAP, MAIN = 18, 16
SPARE = CAP - MAIN
EX_DEV = 2
BF, F32, I32 = jnp.bfloat16, jnp.float32, jnp.int32
VMEM = 60 * 1024 * 1024


def block_rows(n):
    return 2 * n * MAIN + 8


def row_slots(n, shard, array, offset_rows=0):
    r = lax.broadcasted_iota(I32, (block_rows(n), 1), 0)
    main = n * MAIN
    base = array * main + shard * MAIN
    spare = 2 * main + array * SPARE * n + shard * SPARE
    slot = jnp.where((r >= base) & (r < base + MAIN), r - base, -9)
    return jnp.where((r >= spare) & (r < spare + SPARE), MAIN + r - spare, slot)


def expert_keys(routes, ids):
    masks = [jnp.max(jnp.where(routes == e, 1.0, 0.0), axis=0, keepdims=True) for e in ids]
    mask = jnp.concatenate(masks, axis=0)
    t = mask.shape[1]
    before = lax.broadcasted_iota(I32, (t, t), 0) < lax.broadcasted_iota(I32, (t, t), 1)
    tri = jnp.where(before, 1.0, 0.0).astype(BF)
    rank = jnp.dot(mask.astype(BF), tri, preferred_element_type=F32)
    return jnp.where(mask > 0, rank, -1.0)


def dispatch(shard_refs, ids, tok_dev):
    n = len(shard_refs)
    rows = block_rows(n)
    d = shard_refs[0][0].shape[1]
    flat = [a for s in shard_refs for a in s]
    lens = [len(s) for s in shard_refs]

    def kernel(ids_ref, *refs):
        out_ref = refs[-1]
        eid = [ids_ref[j].astype(F32) for j in range(NJ)]
        acc, at = None, 0
        for a in range(n):
            shard = refs[at : at + lens[a]]
            at += lens[a]
            last = shard[-1]
            routes = last[last.shape[0] - 16 :, 0:tok_dev].astype(F32)[0:8]
            keys = expert_keys(routes, eid)
            parts = []
            for array in range(2):
                slots = row_slots(n, a, array).astype(F32)
                hot = [jnp.where(keys[j : j + 1] == slots, 1.0, 0.0) for j in range(NJ)]
                parts.append(jnp.concatenate(hot, axis=0))
            if len(shard) == 1:
                hot = jnp.concatenate(parts, axis=1).astype(BF)
                got = jnp.dot(hot, shard[0][0 : 2 * tok_dev, :], preferred_element_type=F32)
            else:
                got = jnp.dot(parts[0].astype(BF), shard[0][...], preferred_element_type=F32)
                got += jnp.dot(parts[1].astype(BF), shard[1][0:tok_dev, :], preferred_element_type=F32)
            acc = got if acc is None else acc + got
        for j in range(NJ):
            out_ref[j] = acc[j * rows : (j + 1) * rows].astype(BF)

    return pl.pallas_call(
        kernel,
        out_shape=jax.ShapeDtypeStruct((NJ, rows, d), BF),
        in_specs=[pl.BlockSpec(memory_space=pltpu.SMEM)] + [pl.BlockSpec(a.shape, lambda: (0, 0)) for a in flat],
        out_specs=pl.BlockSpec((NJ, rows, d), lambda: (0, 0, 0)),
        compiler_params=pltpu.CompilerParams(vmem_limit_bytes=VMEM),
    )(ids, *flat)


def expert(recv, n, w_gate, w_up, w_down, proj_in, proj_out):
    _, rows, d = recv.shape
    ff = w_gate.shape[1]
    r = proj_in.shape[0]
    chunk = 256
    main = n * MAIN
    m = NJ * main + NJ * 8
    contract = (((1,), (1,)), ((), ()))

    def kernel(x_ref, wg_ref, wu_ref, wd_ref, pi_ref, po_ref, out_ref, xs, cs, acc):
        f = pl.program_id(0)

        @pl.when(f == 0)
        def _():
            for j in range(NJ):
                xs[j * main : (j + 1) * main, :] = x_ref[j, 0:main, :]
                cs[j * main : (j + 1) * main, :] = x_ref[j, main : 2 * main, :]
            spare = [x_ref[j, 2 * main : 2 * main + 8, :].astype(F32) for j in range(NJ)]
            spare = jnp.concatenate(spare, axis=0).astype(BF)
            xs[NJ * main :, :] = spare
            cs[NJ * main :, :] = spare
            acc[...] = jnp.zeros_like(acc)

        x = xs[...]
        gate = jnp.dot(x, wg_ref[...], preferred_element_type=F32)
        up = jnp.dot(x, wu_ref[...], preferred_element_type=F32)
        back = lax.dot_general(cs[...], wd_ref[...], contract, preferred_element_type=F32)
        tail = back[NJ * main :]
        tail = jnp.concatenate([tail[2 * n :], tail[: 2 * n]], axis=0)
        back = jnp.concatenate([back[: NJ * main], tail], axis=0)
        sig = jax.nn.sigmoid(gate)
        hidden = (gate * sig * up).astype(BF)
        delta = (back * up * sig * (1.0 + gate * (1.0 - sig))).astype(BF)
        acc[:, 0:r] += lax.dot_general(hidden, pi_ref[...], contract, preferred_element_type=F32)
        acc[:, r:] += lax.dot_general(delta, po_ref[...], contract, preferred_element_type=F32)

        @pl.when(f == ff // chunk - 1)
        def _():
            for j in range(NJ):
                over = acc[NJ * main + 8 * j : NJ * main + 8 * j + 8]
                pieces = []
                for a in range(n):
                    lo = j * main + a * MAIN
                    pieces += [acc[lo : lo + MAIN], over]
                out_ref[j] = jnp.concatenate(pieces, axis=0).astype(BF)

    back_rows = n * (MAIN + 8)
    return pl.pallas_call(
        kernel,
        grid=(ff // chunk,),
        out_shape=jax.ShapeDtypeStruct((NJ, back_rows, 2 * r), BF),
        in_specs=[
            pl.BlockSpec((NJ, rows, d), lambda f: (0, 0, 0)),
            pl.BlockSpec((d, chunk), lambda f: (0, f)),
            pl.BlockSpec((d, chunk), lambda f: (0, f)),
            pl.BlockSpec((chunk, d), lambda f: (f, 0)),
            pl.BlockSpec((r, chunk), lambda f: (0, f)),
            pl.BlockSpec((r, chunk), lambda f: (0, f)),
        ],
        out_specs=pl.BlockSpec((NJ, back_rows, 2 * r), lambda f: (0, 0, 0)),
        scratch_shapes=[pltpu.VMEM((m, d), BF), pltpu.VMEM((m, d), BF), pltpu.VMEM((m, 2 * r), F32)],
        compiler_params=pltpu.CompilerParams(vmem_limit_bytes=VMEM),
    )(recv, w_gate, w_up, w_down, proj_in, proj_out)


def outer(ids, pieces, routes_t, weight_t, in_model, out_model, member):
    r = out_model.shape[1] // 2
    part = MAIN + 8
    k = NJ * part
    half = r // 2

    def kernel(ids_ref, routes_ref, weight_ref, im_ref, om_ref, mem_ref, *refs):
        out_ref = refs[-1]
        routes = routes_ref[...].astype(F32)
        weight = weight_ref[...]
        table = jnp.concatenate([im_ref[...], om_ref[...], mem_ref[...]], axis=1)
        lane = lax.broadcasted_iota(I32, (1, 2 * r), 1)
        col = lax.broadcasted_iota(I32, (k, NJ * 2 * r), 1) // (2 * r)
        row = lax.broadcasted_iota(I32, (k, NJ * 2 * r), 0) // part
        own = col == row
        pr = lax.broadcasted_iota(I32, (part, 1), 0)
        for p, (_, n, shard) in enumerate(pieces):
            eid = [ids_ref[p * NJ + j] for j in range(NJ)]
            keys = expert_keys(routes, [e.astype(F32) for e in eid])
            q = pr - MAIN - shard * SPARE
            slots = jnp.where(pr < MAIN, pr, jnp.where((q >= 0) & (q < SPARE), MAIN + q, -9)).astype(F32)
            hot, scale = [], []
            for j in range(NJ):
                h = jnp.where(keys[j : j + 1] == slots, 1.0, 0.0)
                we = jnp.sum(jnp.where(routes == eid[j].astype(F32), weight, 0.0), axis=0, keepdims=True)
                hot.append(h)
                scale.append(jnp.sum(h * we, axis=1, keepdims=True))
            hot = jnp.concatenate(hot, axis=0).astype(BF)
            scale = jnp.concatenate(scale, axis=0)
            sel = jnp.dot(hot, table, preferred_element_type=F32)
            im = sel[:, 0 : 2 * r] * scale
            om = sel[:, 2 * r : 4 * r] * scale
            mem = sel[:, 4 * r : 6 * r]
            ret = refs[p]
            got = [ret[j, shard * part : (shard + 1) * part, :].astype(F32) for j in range(NJ)]
            got = jnp.concatenate(got, axis=0)
            inner = jnp.concatenate([got[:, 0:r], got[:, 0:r]], axis=1) * mem
            outh = jnp.concatenate([got[:, r:], got[:, r:]], axis=1)
            for g, (left, right) in enumerate(((im, outh), (inner, om))):
                wide = jnp.concatenate([right] * NJ, axis=1)
                wide = jnp.where(own, wide, 0.0).astype(BF)
                res = lax.dot_general(
                    left.astype(BF), wide, (((0,), (0,)), ((), ())), preferred_element_type=F32
                )
                for j in range(NJ):
                    for s in range(EX_DEV):
                        even = res[s * r : s * r + half, j * 2 * r : (j + 1) * 2 * r]
                        odd = res[s * r + half : (s + 1) * r, j * 2 * r : (j + 1) * 2 * r]
                        out_ref[s, eid[j], g] = jnp.where(lane < r, even, odd).astype(BF)

    arrays = [a for a, _, _ in pieces]
    vmem = pl.BlockSpec(memory_space=pltpu.VMEM)
    return pl.pallas_call(
        kernel,
        out_shape=jax.ShapeDtypeStruct((EX_DEV, NZ * NJ, 2, half, 2 * r), BF),
        in_specs=[pl.BlockSpec(memory_space=pltpu.SMEM)] + [vmem] * (5 + len(arrays)),
        out_specs=vmem,
        compiler_params=pltpu.CompilerParams(vmem_limit_bytes=VMEM),
    )(ids, routes_t, weight_t, in_model, out_model, member, *arrays)


def along_z(a, k):
    return lax.ppermute(a, "z", [(i, (i + k) % NZ) for i in range(NZ)])


def plane_exchange(a):
    return lax.all_to_all(a, ("x", "c"), split_axis=0, concat_axis=0, tiled=True)


def shards(
    tokens, cotangent, routes, route_weight, example_ids, w_gate, w_up, w_down, proj_model, proj_hidden
):
    tok_dev, d = tokens.shape
    r = proj_model.shape[0]
    z = lax.axis_index("z")
    j = jnp.arange(NJ, dtype=I32)
    plane = lambda zz: (j // NC) * (NZ * NC) + zz * NC + j % NC
    here = plane(z)

    routes_t = routes.T
    weight_t = route_weight.T
    extra = jnp.pad(routes_t.astype(BF), ((0, 8), (0, d - tok_dev)))
    own = jnp.concatenate([tokens, cotangent, extra], axis=0)
    split = tok_dev

    order = lambda p: jnp.concatenate([p[0::2], p[1::2]], axis=0)
    proj_in, proj_out = order(proj_hidden), proj_hidden
    wg, wu, wd = w_gate[0], w_up[0], w_down[0]

    fwd = back = own
    shard_steps = [([(own,)], [0])]
    for s in (1, 2, 3):
        fwd, back = along_z(fwd, 1), along_z(back, -1)
        shard_steps.append(([(fwd,), (back,)], [-s, s]))
    top, bottom = along_z(fwd[:split], 1), along_z(back[split:], -1)
    shard_steps.append(([(top, bottom)], [4]))

    pieces, ids = [], []
    for refs, dist in shard_steps:
        n = len(refs)
        got = plane_exchange(dispatch(refs, here, tok_dev))
        ret = plane_exchange(expert(got, n, wg, wu, wd, proj_in, proj_out))
        for a, k in enumerate(dist):
            pieces.append((ret if k == 0 else along_z(ret, k), n, a))
            ids.append(plane((z - k) % NZ))

    dot = lambda a, p: lax.dot_general(a, p, (((1,), (1,)), ((), ())), preferred_element_type=F32)
    in_model = dot(tokens, order(proj_model)).astype(BF)
    out_model = dot(cotangent, proj_model).astype(BF)
    lanes = jnp.arange(2 * r, dtype=I32)[None, :] // r
    member = (example_ids[:, None] == lanes).astype(BF)
    in_model = jnp.concatenate([in_model, in_model], axis=1) * member
    out_model = jnp.concatenate([out_model, out_model], axis=1)
    out = outer(jnp.concatenate(ids), pieces, routes_t, weight_t, in_model, out_model, member)
    return out.reshape(EX_DEV, NZ * NJ, 2, r * r)


def solution(mesh):
    dp = mesh.shape["dp"]
    torus = Mesh(mesh.devices.reshape(dp, NX, NZ, NC), ("dp", "x", "z", "c"))
    part, ex = ("dp", "x", "z", "c"), ("x", "z", "c")
    placed = (
        P(part, None),
        P(part, None),
        P(part, None),
        P(part, None),
        P(part),
        P(ex, None, None),
        P(ex, None, None),
        P(ex, None, None),
        P(),
        P(),
    )
    return jax.shard_map(
        shards, mesh=torus, in_specs=placed, out_specs=P(part, None, None, None), check_vma=False
    )
```

```python
import jax
import jax.numpy as jnp
from jax import lax
from jax.experimental import pallas as pl
from jax.experimental.pallas import tpu as pltpu
from jax.sharding import Mesh
from jax.sharding import PartitionSpec as P

NX, NZ, NC = 4, 8, 2
NJ = NX * NC
CAP, MAIN = 18, 16
SPARE = CAP - MAIN
EX_DEV = 2
BF, F32, I32 = jnp.bfloat16, jnp.float32, jnp.int32
VMEM = 40 * 1024 * 1024
LONG = pl.CostEstimate(flops=int(4e10), bytes_accessed=int(12e6), transcendentals=0)


def block_rows(n):
    return 2 * n * MAIN + 8


def row_slots(n, shard, array, offset_rows=0):
    r = lax.broadcasted_iota(I32, (block_rows(n), 1), 0)
    main = n * MAIN
    base = array * main + shard * MAIN
    spare = 2 * main + array * SPARE * n + shard * SPARE
    slot = jnp.where((r >= base) & (r < base + MAIN), r - base, -9)
    return jnp.where((r >= spare) & (r < spare + SPARE), MAIN + r - spare, slot)


def expert_keys(routes, ids):
    masks = [jnp.max(jnp.where(routes == e, 1.0, 0.0), axis=0, keepdims=True) for e in ids]
    mask = jnp.concatenate(masks, axis=0)
    t = mask.shape[1]
    before = lax.broadcasted_iota(I32, (t, t), 0) < lax.broadcasted_iota(I32, (t, t), 1)
    tri = jnp.where(before, 1.0, 0.0).astype(BF)
    rank = jnp.dot(mask.astype(BF), tri, preferred_element_type=F32)
    return jnp.where(mask > 0, rank, -1.0)


def dispatch(shard_refs, ids, tok_dev, after=()):
    n = len(shard_refs)
    rows = block_rows(n)
    d = shard_refs[0][0].shape[1]
    cols = d // 4
    flat = [a for s in shard_refs for a in s]
    lens = [len(s) for s in shard_refs]

    def kernel(ids_ref, *refs):
        hot_ref, out_ref = refs[-1], refs[-2]
        shards_of, at = [], 0
        for a in range(n):
            shards_of.append(refs[at : at + lens[a]])
            at += lens[a]

        @pl.when(pl.program_id(0) == 0)
        def _():
            eid = [ids_ref[j].astype(F32) for j in range(NJ)]
            for a in range(n):
                last = shards_of[a][-1]
                routes = last[last.shape[0] - 16 :, 0:tok_dev].astype(F32)[0:8]
                keys = expert_keys(routes, eid)
                for array in range(2):
                    slots = row_slots(n, a, array).astype(F32)
                    hot = [jnp.where(keys[j : j + 1] == slots, 1.0, 0.0) for j in range(NJ)]
                    hot = jnp.concatenate(hot, axis=0).astype(BF)
                    hot_ref[a, :, array * tok_dev : (array + 1) * tok_dev] = hot

        acc = None
        for a in range(n):
            shard = shards_of[a]
            if len(shard) == 1:
                got = jnp.dot(hot_ref[a], shard[0][0 : 2 * tok_dev, :], preferred_element_type=F32)
            else:
                got = jnp.dot(hot_ref[a, :, 0:tok_dev], shard[0][...], preferred_element_type=F32)
                got += jnp.dot(
                    hot_ref[a, :, tok_dev:], shard[1][0:tok_dev, :], preferred_element_type=F32
                )
            acc = got if acc is None else acc + got
        for j in range(NJ):
            out_ref[j] = acc[j * rows : (j + 1) * rows].astype(BF)

    return pl.pallas_call(
        kernel,
        name="dispatch",
        grid=(d // cols,),
        out_shape=jax.ShapeDtypeStruct((NJ, rows, d), BF),
        in_specs=[pl.BlockSpec(memory_space=pltpu.SMEM)]
        + [pl.BlockSpec((a.shape[0], cols), lambda i: (0, i)) for a in flat]
        + [pl.BlockSpec(memory_space=pl.ANY)] * len(after),
        out_specs=pl.BlockSpec((NJ, rows, cols), lambda i: (0, 0, i)),
        scratch_shapes=[pltpu.VMEM((n, NJ * rows, 2 * tok_dev), BF)],
        compiler_params=pltpu.CompilerParams(vmem_limit_bytes=VMEM),
    )(ids, *flat, *after)


def expert(recv, n, w_gate, w_up, w_down, proj_in, proj_out):
    _, rows, d = recv.shape
    ff = w_gate.shape[1]
    r = proj_in.shape[0]
    chunk = 256
    main = n * MAIN
    m = NJ * main + NJ * 8
    contract = (((1,), (1,)), ((), ()))

    def kernel(x_ref, wg_ref, wu_ref, wd_ref, pi_ref, po_ref, out_ref, xs, cs, acc):
        f = pl.program_id(0)

        @pl.when(f == 0)
        def _():
            for j in range(NJ):
                xs[j * main : (j + 1) * main, :] = x_ref[j, 0:main, :]
                cs[j * main : (j + 1) * main, :] = x_ref[j, main : 2 * main, :]
            spare = [x_ref[j, 2 * main : 2 * main + 8, :].astype(F32) for j in range(NJ)]
            spare = jnp.concatenate(spare, axis=0).astype(BF)
            xs[NJ * main :, :] = spare
            cs[NJ * main :, :] = spare
            acc[...] = jnp.zeros_like(acc)

        x = xs[...]
        gate = jnp.dot(x, wg_ref[...], preferred_element_type=F32)
        up = jnp.dot(x, wu_ref[...], preferred_element_type=F32)
        back = lax.dot_general(cs[...], wd_ref[...], contract, preferred_element_type=F32)
        tail = back[NJ * main :]
        tail = jnp.concatenate([tail[2 * n :], tail[: 2 * n]], axis=0)
        back = jnp.concatenate([back[: NJ * main], tail], axis=0)
        sig = jax.nn.sigmoid(gate)
        hidden = (gate * sig * up).astype(BF)
        delta = (back * up * sig * (1.0 + gate * (1.0 - sig))).astype(BF)
        acc[:, 0:r] += lax.dot_general(hidden, pi_ref[...], contract, preferred_element_type=F32)
        acc[:, r:] += lax.dot_general(delta, po_ref[...], contract, preferred_element_type=F32)

        @pl.when(f == ff // chunk - 1)
        def _():
            for j in range(NJ):
                over = acc[NJ * main + 8 * j : NJ * main + 8 * j + 8]
                pieces = []
                for a in range(n):
                    lo = j * main + a * MAIN
                    pieces += [acc[lo : lo + MAIN], over]
                out_ref[j] = jnp.concatenate(pieces, axis=0).astype(BF)

    back_rows = n * (MAIN + 8)
    return pl.pallas_call(
        kernel,
        name="expert",
        cost_estimate=LONG,
        grid=(ff // chunk,),
        out_shape=jax.ShapeDtypeStruct((NJ, back_rows, 2 * r), BF),
        in_specs=[
            pl.BlockSpec((NJ, rows, d), lambda f: (0, 0, 0)),
            pl.BlockSpec((d, chunk), lambda f: (0, f)),
            pl.BlockSpec((d, chunk), lambda f: (0, f)),
            pl.BlockSpec((chunk, d), lambda f: (f, 0)),
            pl.BlockSpec((r, chunk), lambda f: (0, f)),
            pl.BlockSpec((r, chunk), lambda f: (0, f)),
        ],
        out_specs=pl.BlockSpec((NJ, back_rows, 2 * r), lambda f: (0, 0, 0)),
        scratch_shapes=[pltpu.VMEM((m, d), BF), pltpu.VMEM((m, d), BF), pltpu.VMEM((m, 2 * r), F32)],
        compiler_params=pltpu.CompilerParams(vmem_limit_bytes=VMEM),
    )(recv, w_gate, w_up, w_down, proj_in, proj_out)


def features(tokens, cotangent, proj_in, proj_out):
    t = tokens.shape[0]
    r = proj_in.shape[0]
    contract = (((1,), (1,)), ((), ()))

    def kernel(x_ref, c_ref, pi_ref, po_ref, out_ref):
        out_ref[:, 0:r] = lax.dot_general(x_ref[...], pi_ref[...], contract, preferred_element_type=F32).astype(BF)
        out_ref[:, r:] = lax.dot_general(c_ref[...], po_ref[...], contract, preferred_element_type=F32).astype(BF)

    return pl.pallas_call(
        kernel,
        name="features",
        cost_estimate=LONG,
        out_shape=jax.ShapeDtypeStruct((t, 2 * r), BF),
        compiler_params=pltpu.CompilerParams(vmem_limit_bytes=VMEM),
    )(tokens, cotangent, proj_in, proj_out)


def outer(ids, pieces, routes_t, weight_t, example, table, into=None):
    r = table.shape[1] // 2
    part = MAIN + 8
    k = NJ * part
    half = r // 2

    def kernel(ids_ref, routes_ref, weight_ref, ex_ref, table_ref, *refs):
        refs = refs[: len(pieces)] + refs[len(pieces) + (into is not None) :]
        if into is None:
            out_ref = refs[len(pieces)]
        else:
            final_ref, out_ref, sem = refs[len(pieces) :]
        routes = routes_ref[...].astype(F32)
        weight = weight_ref[...]
        example = ex_ref[...].astype(F32)
        lane = lax.broadcasted_iota(I32, (1, 2 * r), 1)
        col = lax.broadcasted_iota(I32, (k, NJ * 2 * r), 1) // (2 * r)
        row = lax.broadcasted_iota(I32, (k, NJ * 2 * r), 0) // part
        own = col == row
        pr = lax.broadcasted_iota(I32, (part, 1), 0)
        for p, (_, shard) in enumerate(pieces):
            eid = [ids_ref[p * NJ + j] for j in range(NJ)]
            keys = expert_keys(routes, [e.astype(F32) for e in eid])
            q = pr - MAIN - shard * SPARE
            slots = jnp.where(pr < MAIN, pr, jnp.where((q >= 0) & (q < SPARE), MAIN + q, -9)).astype(F32)
            hot, scale, held, second = [], [], [], []
            for j in range(NJ):
                h = jnp.where(keys[j : j + 1] == slots, 1.0, 0.0)
                we = jnp.sum(jnp.where(routes == eid[j].astype(F32), weight, 0.0), axis=0, keepdims=True)
                hot.append(h)
                scale.append(jnp.sum(h * we, axis=1, keepdims=True))
                held.append(jnp.sum(h, axis=1, keepdims=True))
                second.append(jnp.sum(h * example, axis=1, keepdims=True))
            hot = jnp.concatenate(hot, axis=0).astype(BF)
            scale = jnp.concatenate(scale, axis=0)
            held = jnp.concatenate(held, axis=0)
            second = jnp.concatenate(second, axis=0)
            mem = jnp.where(lane < r, held - second, second)
            sel = jnp.dot(hot, table_ref[...], preferred_element_type=F32) * scale
            got = jnp.concatenate([refs[p][j].astype(F32) for j in range(NJ)], axis=0)
            twice = lambda v: jnp.concatenate([v, v], axis=1)
            im = twice(sel[:, 0:r]) * mem
            om = twice(sel[:, r:])
            inner = twice(got[:, 0:r]) * mem
            outh = twice(got[:, r:])
            for g, (left, right) in enumerate(((im, outh), (inner, om))):
                wide = jnp.concatenate([right] * NJ, axis=1)
                wide = jnp.where(own, wide, 0.0).astype(BF)
                res = lax.dot_general(
                    left.astype(BF), wide, (((0,), (0,)), ((), ())), preferred_element_type=F32
                )
                for j in range(NJ):
                    for s in range(EX_DEV):
                        even = res[s * r : s * r + half, j * 2 * r : (j + 1) * 2 * r]
                        odd = res[s * r + half : (s + 1) * r, j * 2 * r : (j + 1) * 2 * r]
                        block = jnp.where(lane < r, even, odd).astype(BF)
                        if into is None:
                            out_ref[s, eid[j], g] = block
                        else:
                            out_ref[s, j, g] = block
            if into is not None:
                copies = []
                for s in range(EX_DEV):
                    for x in range(NX):
                        src = out_ref.at[s, pl.ds(x * NC, NC)]
                        dst = final_ref.at[s, pl.ds(eid[x * NC], NC)]
                        copies.append(pltpu.make_async_copy(src, dst, sem.at[s * NX + x]))
                for c in copies:
                    c.start()
                for c in copies:
                    c.wait()

    arrays = [a for a, _ in pieces]
    vmem = pl.BlockSpec(memory_space=pltpu.VMEM)
    extra, out_specs, scratch, alias = [], vmem, [], {}
    if into is not None:
        assert len(pieces) == 1
        extra, out_specs = [into], pl.BlockSpec(memory_space=pl.ANY)
        scratch = [pltpu.VMEM((EX_DEV, NJ, 2, half, 2 * r), BF), pltpu.SemaphoreType.DMA((EX_DEV * NX,))]
        alias = {5 + len(arrays): 0}
    return pl.pallas_call(
        kernel,
        name="outer",
        out_shape=jax.ShapeDtypeStruct((EX_DEV, NZ * NJ, 2, half, 2 * r), BF),
        in_specs=[pl.BlockSpec(memory_space=pltpu.SMEM)]
        + [vmem] * (4 + len(arrays))
        + [pl.BlockSpec(memory_space=pl.ANY)] * len(extra),
        out_specs=out_specs,
        scratch_shapes=scratch,
        input_output_aliases=alias,
        compiler_params=pltpu.CompilerParams(vmem_limit_bytes=VMEM),
    )(ids, routes_t, weight_t, example, table, *arrays, *extra)


def along_z(a, k):
    return lax.ppermute(a, "z", [(i, (i + k) % NZ) for i in range(NZ)])


def plane_exchange(a):
    return lax.all_to_all(a, ("x", "c"), split_axis=0, concat_axis=0, tiled=True)


def shards(
    tokens, cotangent, routes, route_weight, example_ids, w_gate, w_up, w_down, proj_model, proj_hidden
):
    tok_dev, d = tokens.shape
    r = proj_model.shape[0]
    z = lax.axis_index("z")
    j = jnp.arange(NJ, dtype=I32)
    plane = lambda zz: (j // NC) * (NZ * NC) + zz * NC + j % NC
    here = plane(z)

    routes_t = routes.T
    weight_t = route_weight.T
    extra = jnp.pad(routes_t.astype(BF), ((0, 8), (0, d - tok_dev)))
    own = jnp.concatenate([tokens, cotangent, extra], axis=0)
    split = tok_dev

    order = lambda p: jnp.concatenate([p[0::2], p[1::2]], axis=0)
    proj_in, proj_out = order(proj_hidden), proj_hidden
    wg, wu, wd = w_gate[0], w_up[0], w_down[0]

    fwd = back = own
    shard_steps = [([(own,)], [0])]
    for s in (1, 2, 3):
        fwd, back = along_z(fwd, 1), along_z(back, -1)
        shard_steps.append(([(fwd,), (back,)], [-s, s]))
    top, bottom = along_z(fwd[:split], 1), along_z(back[split:], -1)
    shard_steps.append(([(top, bottom)], [4]))

    table = features(tokens, cotangent, order(proj_model), proj_model)
    rets = []
    for i, (refs, dist) in enumerate(shard_steps):
        after = rets[i - 2 : i - 1] if i >= 2 else [table] * i
        got = plane_exchange(dispatch(refs, here, tok_dev, after))
        rets.append(expert(got, len(refs), wg, wu, wd, proj_in, proj_out))

    part = MAIN + 8
    most = plane_exchange(jnp.concatenate(rets[:-1], axis=1))
    last, most = lax.optimization_barrier((rets[-1], most))
    last = along_z(plane_exchange(last), 4)
    pieces, at = [], 0
    for refs, dist in shard_steps[:-1]:
        for a, k in enumerate(dist):
            rows = most[:, at : at + part]
            pieces.append((rows if k == 0 else along_z(rows, k), a))
            at += part
    ids = [plane((z - k) % NZ) for _, dist in shard_steps for k in dist]
    mine = (routes_t, weight_t, example_ids[None, :], table)
    out = outer(jnp.concatenate(ids[:-1]), pieces, *mine)
    out = outer(ids[-1], [(last, 0)], *mine, into=out)
    return out.reshape(EX_DEV, NZ * NJ, 2, r * r)


def solution(mesh):
    dp = mesh.shape["dp"]
    torus = Mesh(mesh.devices.reshape(dp, NX, NZ, NC), ("dp", "x", "z", "c"))
    part, ex = ("dp", "x", "z", "c"), ("x", "z", "c")
    placed = (
        P(part, None),
        P(part, None),
        P(part, None),
        P(part, None),
        P(part),
        P(ex, None, None),
        P(ex, None, None),
        P(ex, None, None),
        P(),
        P(),
    )
    return jax.shard_map(
        shards, mesh=torus, in_specs=placed, out_specs=P(part, None, None, None), check_vma=False
    )
```

```python
import jax
import jax.numpy as jnp
from jax import lax
from jax.experimental import pallas as pl
from jax.experimental.pallas import tpu as pltpu
from jax.sharding import Mesh
from jax.sharding import PartitionSpec as P

NX, NZ, NC = 4, 8, 2
NJ = NX * NC
STEPS_X = (0, 1, 3, 2)
CAP, MAIN = 18, 16
SPARE = CAP - MAIN
EX_DEV = 2
BF, F32, I32 = jnp.bfloat16, jnp.float32, jnp.int32
VMEM = 40 * 1024 * 1024
LONG = pl.CostEstimate(flops=int(4e10), bytes_accessed=int(12e6), transcendentals=0)


def block_rows(n):
    return 2 * n * MAIN + 8


def row_slots(n, shard, array, offset_rows=0):
    r = lax.broadcasted_iota(I32, (block_rows(n), 1), 0)
    main = n * MAIN
    base = array * main + shard * MAIN
    spare = 2 * main + array * SPARE * n + shard * SPARE
    slot = jnp.where((r >= base) & (r < base + MAIN), r - base, -9)
    return jnp.where((r >= spare) & (r < spare + SPARE), MAIN + r - spare, slot)


def expert_keys(routes, ids):
    masks = [jnp.max(jnp.where(routes == e, 1.0, 0.0), axis=0, keepdims=True) for e in ids]
    mask = jnp.concatenate(masks, axis=0)
    t = mask.shape[1]
    before = lax.broadcasted_iota(I32, (t, t), 0) < lax.broadcasted_iota(I32, (t, t), 1)
    tri = jnp.where(before, 1.0, 0.0).astype(BF)
    rank = jnp.dot(mask.astype(BF), tri, preferred_element_type=F32)
    return jnp.where(mask > 0, rank, -1.0)


def dispatch(shard_refs, ids, tok_dev, after=()):
    n = len(shard_refs)
    rows = block_rows(n)
    d = shard_refs[0][0].shape[1]
    cols = d // 4
    flat = [a for s in shard_refs for a in s]
    lens = [len(s) for s in shard_refs]

    def kernel(ids_ref, *refs):
        hot_ref, out_refs = refs[-1], refs[-1 - NX : -1]
        shards_of, at = [], 0
        for a in range(n):
            shards_of.append(refs[at : at + lens[a]])
            at += lens[a]

        @pl.when(pl.program_id(0) == 0)
        def _():
            eid = [ids_ref[j].astype(F32) for j in range(NJ)]
            for a in range(n):
                last = shards_of[a][-1]
                routes = last[last.shape[0] - 16 :, 0:tok_dev].astype(F32)[0:8]
                keys = expert_keys(routes, eid)
                for array in range(2):
                    slots = row_slots(n, a, array).astype(F32)
                    hot = [jnp.where(keys[j : j + 1] == slots, 1.0, 0.0) for j in range(NJ)]
                    hot = jnp.concatenate(hot, axis=0).astype(BF)
                    hot_ref[a, :, array * tok_dev : (array + 1) * tok_dev] = hot

        acc = None
        for a in range(n):
            shard = shards_of[a]
            if len(shard) == 1:
                got = jnp.dot(hot_ref[a], shard[0][0 : 2 * tok_dev, :], preferred_element_type=F32)
            else:
                got = jnp.dot(hot_ref[a, :, 0:tok_dev], shard[0][...], preferred_element_type=F32)
                got += jnp.dot(
                    hot_ref[a, :, tok_dev:], shard[1][0:tok_dev, :], preferred_element_type=F32
                )
            acc = got if acc is None else acc + got
        for j in range(NJ):
            out_refs[j // NC][j % NC] = acc[j * rows : (j + 1) * rows].astype(BF)

    return pl.pallas_call(
        kernel,
        name="dispatch",
        grid=(d // cols,),
        out_shape=[jax.ShapeDtypeStruct((NC, rows, d), BF)] * NX,
        in_specs=[pl.BlockSpec(memory_space=pltpu.SMEM)]
        + [pl.BlockSpec((a.shape[0], cols), lambda i: (0, i)) for a in flat]
        + [pl.BlockSpec(memory_space=pl.ANY)] * len(after),
        out_specs=[pl.BlockSpec((NC, rows, cols), lambda i: (0, 0, i))] * NX,
        scratch_shapes=[pltpu.VMEM((n, NJ * rows, 2 * tok_dev), BF)],
        compiler_params=pltpu.CompilerParams(vmem_limit_bytes=VMEM),
    )(ids, *flat, *after)


def expert(core, recv, n, weights, proj_in, proj_out, split, after=()):
    _, rows, d = recv[0].shape
    ff = weights[0].shape[2]
    r = proj_in.shape[0]
    chunk = 256
    chunks = ff // chunk
    n_w = len(weights)
    main = n * MAIN
    base = NX * main
    m = base + NX * 8
    part = MAIN + 8
    contract = (((1,), (1,)), ((), ()))
    n_out = NX if split else n

    def kernel(core_ref, *refs):
        x_refs = refs[:NX]
        gate_w, up_w, down_w = refs[NX : NX + n_w]
        pi_ref, po_ref = refs[NX + n_w : NX + n_w + 2]
        refs = refs[NX + n_w + 2 + len(after) :]
        out_refs = refs[:n_out]
        wg, wu, wd, xs, cs, sem = refs[n_out:]

        def copies(k, f):
            span = pl.ds(f * chunk, chunk)
            who = core_ref[k]
            return (
                pltpu.make_async_copy(gate_w.at[who, :, span], wg.at[k, f], sem.at[k, f, 0]),
                pltpu.make_async_copy(up_w.at[who, :, span], wu.at[k, f], sem.at[k, f, 1]),
                pltpu.make_async_copy(down_w.at[who, span, :], wd.at[k, f], sem.at[k, f, 2]),
            )

        for k in range(NC):
            for f in range(chunks):
                for c in copies(k, f):
                    c.start()
        for k in range(NC):
            for i in range(NX):
                xs[k, i * main : (i + 1) * main, :] = x_refs[i][k, 0:main, :]
                cs[k, i * main : (i + 1) * main, :] = x_refs[i][k, main : 2 * main, :]
            spare = [x_refs[i][k, 2 * main : 2 * main + 8, :].astype(F32) for i in range(NX)]
            spare = jnp.concatenate(spare, axis=0).astype(BF)
            xs[k, base:, :] = spare
            cs[k, base:, :] = spare
        for k in range(NC):
            inner, outer_ = None, None
            for f in range(chunks):
                for c in copies(k, f):
                    c.wait()
                x = xs[k]
                gate = jnp.dot(x, wg[k, f], preferred_element_type=F32)
                up = jnp.dot(x, wu[k, f], preferred_element_type=F32)
                back = lax.dot_general(cs[k], wd[k, f], contract, preferred_element_type=F32)
                tail = back[base:]
                tail = jnp.concatenate([tail[2 * n :], tail[: 2 * n]], axis=0)
                back = jnp.concatenate([back[:base], tail], axis=0)
                sig = jax.nn.sigmoid(gate)
                hidden = (gate * sig * up).astype(BF)
                delta = (back * up * sig * (1.0 + gate * (1.0 - sig))).astype(BF)
                span = slice(f * chunk, (f + 1) * chunk)
                hid = lax.dot_general(hidden, pi_ref[:, span], contract, preferred_element_type=F32)
                dlt = lax.dot_general(delta, po_ref[:, span], contract, preferred_element_type=F32)
                inner = hid if inner is None else inner + hid
                outer_ = dlt if outer_ is None else outer_ + dlt
            acc = jnp.concatenate([inner, outer_], axis=1)
            for i in range(NX):
                over = acc[base + 8 * i : base + 8 * i + 8]
                for a in range(n):
                    lo = i * main + a * MAIN
                    block = jnp.concatenate([acc[lo : lo + MAIN], over], axis=0).astype(BF)
                    if split:
                        out_refs[i][k] = block
                    else:
                        out_refs[a][core_ref[NC + i], k] = block

    lead = (NC,) if split else (NX, NC)
    vmem, hbm = pl.BlockSpec(memory_space=pltpu.VMEM), pl.BlockSpec(memory_space=pl.ANY)
    return pl.pallas_call(
        kernel,
        name="expert",
        cost_estimate=LONG,
        out_shape=[jax.ShapeDtypeStruct(lead + (part, 2 * r), BF)] * n_out,
        in_specs=[pl.BlockSpec(memory_space=pltpu.SMEM)] + [vmem] * NX + [hbm] * n_w + [vmem] * 2 + [hbm] * len(after),
        out_specs=[vmem] * n_out,
        scratch_shapes=[
            pltpu.VMEM((NC, chunks, d, chunk), BF),
            pltpu.VMEM((NC, chunks, d, chunk), BF),
            pltpu.VMEM((NC, chunks, chunk, d), BF),
            pltpu.VMEM((NC, m, d), BF),
            pltpu.VMEM((NC, m, d), BF),
            pltpu.SemaphoreType.DMA((NC, chunks, 3)),
        ],
        compiler_params=pltpu.CompilerParams(vmem_limit_bytes=VMEM),
    )(core, *recv, *weights, proj_in, proj_out, *after)


def collect(spots, rets):
    _, nc, part, width = rets[0].shape

    def kernel(spots_ref, *refs):
        for i in range(NX):
            for n, ref in enumerate(refs[:-1]):
                refs[-1][i * NZ + spots_ref[n]] = ref[i]
            refs[-1][i * NZ + spots_ref[len(rets)]] = jnp.zeros((nc, part, width), BF)

    vmem = pl.BlockSpec(memory_space=pltpu.VMEM)
    return pl.pallas_call(
        kernel,
        name="collect",
        out_shape=jax.ShapeDtypeStruct((NX * NZ, nc, part, width), BF),
        in_specs=[pl.BlockSpec(memory_space=pltpu.SMEM)] + [vmem] * len(rets),
        out_specs=vmem,
    )(spots, *rets)


def features(tokens, cotangent, proj_in, proj_out):
    t = tokens.shape[0]
    r = proj_in.shape[0]
    contract = (((1,), (1,)), ((), ()))

    def kernel(x_ref, c_ref, pi_ref, po_ref, out_ref):
        out_ref[:, 0:r] = lax.dot_general(x_ref[...], pi_ref[...], contract, preferred_element_type=F32).astype(BF)
        out_ref[:, r:] = lax.dot_general(c_ref[...], po_ref[...], contract, preferred_element_type=F32).astype(BF)

    return pl.pallas_call(
        kernel,
        name="features",
        cost_estimate=LONG,
        out_shape=jax.ShapeDtypeStruct((t, 2 * r), BF),
        compiler_params=pltpu.CompilerParams(vmem_limit_bytes=VMEM),
    )(tokens, cotangent, proj_in, proj_out)


def outer(ids, arrays, place, routes_t, weight_t, example, table, into=None):
    r = table.shape[1] // 2
    part = MAIN + 8
    k = NJ * part
    half = r // 2
    n_in = len(arrays)

    def kernel(ids_ref, routes_ref, weight_ref, ex_ref, table_ref, *refs):
        in_refs, refs = refs[:n_in], refs[n_in:]
        if into is None:
            out_ref = refs[0]
        else:
            final_ref, out_ref, sem = refs[1:]
        routes = routes_ref[...].astype(F32)
        weight = weight_ref[...]
        example = ex_ref[...].astype(F32)
        lane = lax.broadcasted_iota(I32, (1, 2 * r), 1)
        col = lax.broadcasted_iota(I32, (k, NJ * 2 * r), 1) // (2 * r)
        row = lax.broadcasted_iota(I32, (k, NJ * 2 * r), 0) // part
        own = col == row
        pr = lax.broadcasted_iota(I32, (part, 1), 0)
        for p, shard in enumerate(place):
            eid = [ids_ref[p * NJ + j] for j in range(NJ)]
            keys = expert_keys(routes, [e.astype(F32) for e in eid])
            q = pr - MAIN - shard * SPARE
            slots = jnp.where(pr < MAIN, pr, jnp.where((q >= 0) & (q < SPARE), MAIN + q, -9)).astype(F32)
            hot, scale, held, second = [], [], [], []
            for j in range(NJ):
                h = jnp.where(keys[j : j + 1] == slots, 1.0, 0.0)
                we = jnp.sum(jnp.where(routes == eid[j].astype(F32), weight, 0.0), axis=0, keepdims=True)
                hot.append(h)
                scale.append(jnp.sum(h * we, axis=1, keepdims=True))
                held.append(jnp.sum(h, axis=1, keepdims=True))
                second.append(jnp.sum(h * example, axis=1, keepdims=True))
            hot = jnp.concatenate(hot, axis=0).astype(BF)
            scale = jnp.concatenate(scale, axis=0)
            held = jnp.concatenate(held, axis=0)
            second = jnp.concatenate(second, axis=0)
            mem = jnp.where(lane < r, held - second, second)
            sel = jnp.dot(hot, table_ref[...], preferred_element_type=F32) * scale
            if n_in == 1:
                at = ids_ref[len(place) * NJ + p]
                got = [in_refs[0][j // NC * NZ + at, j % NC].astype(F32) for j in range(NJ)]
            else:
                got = [in_refs[j // NC][j % NC].astype(F32) for j in range(NJ)]
            got = jnp.concatenate(got, axis=0)
            twice = lambda v: jnp.concatenate([v, v], axis=1)
            im = twice(sel[:, 0:r]) * mem
            om = twice(sel[:, r:])
            inner = twice(got[:, 0:r]) * mem
            outh = twice(got[:, r:])
            for g, (left, right) in enumerate(((im, outh), (inner, om))):
                wide = jnp.concatenate([right] * NJ, axis=1)
                wide = jnp.where(own, wide, 0.0).astype(BF)
                res = lax.dot_general(
                    left.astype(BF), wide, (((0,), (0,)), ((), ())), preferred_element_type=F32
                )
                for j in range(NJ):
                    for s in range(EX_DEV):
                        even = res[s * r : s * r + half, j * 2 * r : (j + 1) * 2 * r]
                        odd = res[s * r + half : (s + 1) * r, j * 2 * r : (j + 1) * 2 * r]
                        block = jnp.where(lane < r, even, odd).astype(BF)
                        if into is None:
                            out_ref[s, eid[j], g] = block
                        else:
                            out_ref[s, j, g] = block
            if into is not None:
                copies = []
                for s in range(EX_DEV):
                    for j in range(NJ):
                        dst = final_ref.at[s, eid[j]]
                        copies.append(pltpu.make_async_copy(out_ref.at[s, j], dst, sem.at[s * NJ + j]))
                for c in copies:
                    c.start()
                for c in copies:
                    c.wait()

    vmem = pl.BlockSpec(memory_space=pltpu.VMEM)
    extra, out_specs, scratch, alias = [], vmem, [], {}
    if into is not None:
        assert len(place) == 1
        extra, out_specs = [into], pl.BlockSpec(memory_space=pl.ANY)
        scratch = [pltpu.VMEM((EX_DEV, NJ, 2, half, 2 * r), BF), pltpu.SemaphoreType.DMA((EX_DEV * NJ,))]
        alias = {5 + len(arrays): 0}
    return pl.pallas_call(
        kernel,
        name="outer",
        out_shape=jax.ShapeDtypeStruct((EX_DEV, NZ * NJ, 2, half, 2 * r), BF),
        in_specs=[pl.BlockSpec(memory_space=pltpu.SMEM)]
        + [vmem] * (4 + len(arrays))
        + [pl.BlockSpec(memory_space=pl.ANY)] * len(extra),
        out_specs=out_specs,
        scratch_shapes=scratch,
        input_output_aliases=alias,
        compiler_params=pltpu.CompilerParams(vmem_limit_bytes=VMEM),
    )(ids, routes_t, weight_t, example, table, *arrays, *extra)


def ordered(arrays, after):
    whole = pl.BlockSpec(memory_space=pl.ANY)
    return pl.pallas_call(
        lambda *refs: None,
        name="ordered",
        out_shape=[jax.ShapeDtypeStruct(a.shape, a.dtype) for a in arrays],
        in_specs=[whole] * (len(arrays) + len(after)),
        out_specs=[whole] * len(arrays),
        input_output_aliases={i: i for i in range(len(arrays))},
    )(*arrays, *after)


def along_z(a, k):
    return lax.ppermute(a, "z", [(i, (i + k) % NZ) for i in range(NZ)])


def along_x(a, k):
    return a if k == 0 else lax.ppermute(a, "x", [(i, (i + k) % NX) for i in range(NX)])


def along_both(a, kx, kz):
    to = lambda i: (i // NZ + kx) % NX * NZ + (i % NZ + kz) % NZ
    return lax.ppermute(a, ("x", "z"), [(i, to(i)) for i in range(NX * NZ)])


def shards(
    tokens, cotangent, routes, route_weight, example_ids, w_gate, w_up, w_down, proj_model, proj_hidden
):
    tok_dev, d = tokens.shape
    r = proj_model.shape[0]
    x, z, c = (lax.axis_index(axis) for axis in ("x", "z", "c"))
    plane = lambda zz: jnp.stack(
        [(x + k) % NX * (NZ * NC) + zz * NC + (c ^ other) for k in STEPS_X for other in range(NC)]
    )
    here = plane(z)

    routes_t = routes.T
    weight_t = route_weight.T
    extra = jnp.pad(routes_t.astype(BF), ((0, 8), (0, d - tok_dev)))
    own = jnp.concatenate([tokens, cotangent, extra], axis=0)

    order = lambda p: jnp.concatenate([p[0::2], p[1::2]], axis=0)
    proj_in, proj_out = order(proj_hidden), proj_hidden
    weights = [lax.all_gather(w, "c", axis=0, tiled=True) for w in (w_gate, w_up, w_down)]
    table = features(tokens, cotangent, order(proj_model), proj_model)
    sources = [(x - k) % NX for k in STEPS_X]
    core = jnp.stack([c, 1 - c] + sources)

    fwd = back = own
    recvs, rets = [], []
    run_expert = lambda i, after: expert(
        core, recvs[i], len(places[i]), weights, proj_in, proj_out, i == 4, after
    )
    places = [[0], [-1, 1], [-2, 2], [-3, 3], [4]]
    for i, dist in enumerate(places):
        refs = [(own,)]
        if i:
            if i < 4:
                fwd, back = along_z(fwd, 1), along_z(back, -1)
                before = [table] + recvs[0][1:] if i == 1 else [sent[0], rets[i - 2][0]]
                fwd, back = ordered((fwd, back), before)
                refs = [(fwd,), (back,)]
            else:
                refs = [(along_z(fwd[:tok_dev], 1), along_z(back[tok_dev:], -1))]
        after = [] if i < 2 else [rets[i - 2][0]]
        sent = dispatch(refs, here, tok_dev, after)
        recvs.append([along_x(a, k) for a, k in zip(sent, STEPS_X)])
        if i:
            rets.append(run_expert(i - 1, [sent[0]]))

    near = [(k, a, i) for i, dist in enumerate(places[:-1]) for a, k in enumerate(dist)]
    most = collect(jnp.stack([(z + k) % NZ for k, _, _ in near] + [(z + 4) % NZ]), [rets[i][a] for _, a, i in near])
    most = lax.all_to_all(most, ("x", "z"), split_axis=0, concat_axis=0, tiled=True)
    last = run_expert(4, [])
    last = [along_both(a, -k, 4) for a, k in zip(last, STEPS_X)]

    j = jnp.arange(NJ, dtype=I32)
    fixed = lambda zz: (j // NC) * (NZ * NC) + zz * NC + (c ^ (j % NC))
    planes = [(z - k) % NZ for k, _, _ in near]
    ids = jnp.concatenate([fixed(p) for p in planes] + [jnp.stack(planes)])
    mine = (routes_t, weight_t, example_ids[None, :], table)
    out = outer(ids, [most], [a for _, a, _ in near], *mine)
    out = outer(plane((z - 4) % NZ), last, [0], *mine, into=out)
    return out.reshape(EX_DEV, NZ * NJ, 2, r * r)


def solution(mesh):
    dp = mesh.shape["dp"]
    torus = Mesh(mesh.devices.reshape(dp, NX, NZ, NC), ("dp", "x", "z", "c"))
    part, ex = ("dp", "x", "z", "c"), ("x", "z", "c")
    placed = (
        P(part, None),
        P(part, None),
        P(part, None),
        P(part, None),
        P(part),
        P(ex, None, None),
        P(ex, None, None),
        P(ex, None, None),
        P(),
        P(),
    )
    return jax.shard_map(
        shards, mesh=torus, in_specs=placed, out_specs=P(part, None, None, None), check_vma=False
    )
```

```python
import jax
import jax.numpy as jnp
from jax import lax
from jax.experimental import pallas as pl
from jax.experimental.pallas import tpu as pltpu
from jax.sharding import Mesh
from jax.sharding import PartitionSpec as P

NX, NZ, NC = 4, 8, 2
NJ = NX * NC
STEPS_X = (0, 1, 3, 2)
JOINED = (0, 2)
CAP, MAIN = 18, 16
SPARE = CAP - MAIN
EX_DEV = 2
BF, F32, I32 = jnp.bfloat16, jnp.float32, jnp.int32
VMEM = 24 * 1024 * 1024
MARK = pltpu.VMEM((8, 128), F32)
LONG = pl.CostEstimate(flops=int(4e10), bytes_accessed=int(12e6), transcendentals=0)


def in_hbm(arrays):
    return [pltpu.with_memory_space_constraint(a, pltpu.HBM) for a in arrays]


def in_vmem(arrays):
    return [pltpu.with_memory_space_constraint(a, pltpu.VMEM) for a in arrays]


def block_rows(n):
    return 2 * n * MAIN + 8


def row_slots(n, shard, array, offset_rows=0):
    r = lax.broadcasted_iota(I32, (block_rows(n), 1), 0)
    main = n * MAIN
    base = array * main + shard * MAIN
    spare = 2 * main + array * SPARE * n + shard * SPARE
    slot = jnp.where((r >= base) & (r < base + MAIN), r - base, -9)
    return jnp.where((r >= spare) & (r < spare + SPARE), MAIN + r - spare, slot)


def expert_keys(routes, ids):
    masks = [jnp.max(jnp.where(routes == e, 1.0, 0.0), axis=0, keepdims=True) for e in ids]
    mask = jnp.concatenate(masks, axis=0)
    t = mask.shape[1]
    before = lax.broadcasted_iota(I32, (t, t), 0) < lax.broadcasted_iota(I32, (t, t), 1)
    tri = jnp.where(before, 1.0, 0.0).astype(BF)
    rank = jnp.dot(mask.astype(BF), tri, preferred_element_type=F32)
    return jnp.where(mask > 0, rank, -1.0)


def dispatch(shard_refs, ids, tok_dev, joined, after=()):
    n = len(shard_refs)
    rows = block_rows(n)
    d = shard_refs[0].shape[1]
    chunks = 4
    cols = d // chunks
    n_out, lead = (1, (NX,)) if joined else (NX, ())
    first = 0 if joined else 1

    def kernel(ids_ref, *refs):
        ins, refs = refs[: n], refs[n + len(after) :]
        outs, mark_ref, refs = refs[:n_out], refs[n_out], refs[n_out + 1 :]
        held, (sent, hot_ref, near, in_sem, out_sem, near_sem) = refs[:n], refs[n:]

        def span(q):
            return pl.ds(q * cols, cols)

        def copy_in(i, q):
            return pltpu.make_async_copy(ins[i].at[:, span(q)], held[i].at[:, span(q)], in_sem.at[i, q])

        def copy_out(i, q):
            to = outs[0].at[ids_ref[NJ + i]] if joined else outs[i]
            src = sent.at[pl.ds(i * NC, NC), :, span(q)]
            return pltpu.make_async_copy(src, to.at[:, :, span(q)], out_sem.at[i, q])

        def copy_near(i):
            src = ins[i].at[pl.ds(2 * tok_dev, 16), pl.ds(0, tok_dev)]
            return pltpu.make_async_copy(src, near.at[i], near_sem.at[i])

        for i in range(n):
            copy_near(i).start()
        for q in range(chunks):
            for i in range(n):
                copy_in(i, q).start()
        mark_ref[...] = jnp.zeros_like(mark_ref)
        eid = [ids_ref[j].astype(F32) for j in range(NJ)]
        for a in range(n):
            copy_near(a).wait()
            keys = expert_keys(near[a].astype(F32)[0:8], eid)
            for array in range(2):
                slots = row_slots(n, a, array).astype(F32)
                hot = [jnp.where(keys[j : j + 1] == slots, 1.0, 0.0) for j in range(NJ)]
                hot = jnp.concatenate(hot, axis=0).astype(BF)
                hot_ref[a, :, array * tok_dev : (array + 1) * tok_dev] = hot
        for q in range(chunks):
            for i in range(n):
                copy_in(i, q).wait()
            here = slice(q * cols, (q + 1) * cols)
            acc = None
            for a in range(n):
                got = jnp.dot(hot_ref[a], held[a][0 : 2 * tok_dev, here], preferred_element_type=F32)
                acc = got if acc is None else acc + got
            for j in range(NJ):
                block = acc[j * rows : (j + 1) * rows].astype(BF)
                if j < NC * first:
                    outs[0][j, :, here] = block
                else:
                    sent[j, :, here] = block
            for i in range(first, NX):
                copy_out(i, q).start()
        for q in range(chunks):
            for i in range(first, NX):
                copy_out(i, q).wait()

    vmem, hbm = pl.BlockSpec(memory_space=pltpu.VMEM), pl.BlockSpec(memory_space=pltpu.HBM)
    return pl.pallas_call(
        kernel,
        name="dispatch",
        out_shape=[pltpu.VMEM((NC, rows, d), BF)] * first
        + [pltpu.HBM(lead + (NC, rows, d), BF)] * (n_out - first)
        + [MARK],
        in_specs=[pl.BlockSpec(memory_space=pltpu.SMEM)] + [hbm] * n + [vmem] * len(after),
        out_specs=[vmem] * first + [hbm] * (n_out - first) + [vmem],
        scratch_shapes=[pltpu.VMEM(a.shape, BF) for a in shard_refs]
        + [
            pltpu.VMEM((NJ, rows, d), BF),
            pltpu.VMEM((n, NJ * rows, 2 * tok_dev), BF),
            pltpu.VMEM((n, 16, tok_dev), BF),
            pltpu.SemaphoreType.DMA((n, chunks)),
            pltpu.SemaphoreType.DMA((NX, chunks)),
            pltpu.SemaphoreType.DMA((n,)),
        ],
        compiler_params=pltpu.CompilerParams(vmem_limit_bytes=VMEM),
    )(ids, *in_hbm(shard_refs), *in_vmem(after))


def expert(spots, recv, n, weights, proj_in, proj_out, into, after=()):
    rows, d = recv[0].shape[-2:]
    n_in = len(recv)
    ff = weights[0].shape[-1]
    r = proj_in.shape[0]
    chunk = 256
    chunks = ff // chunk
    n_w = len(weights)
    main = n * MAIN
    base = NX * main
    m = base + NX * 8
    part = MAIN + 8
    contract = (((1,), (1,)), ((), ()))

    one = into is False
    extra = [] if into is None or one else [into]

    def kernel(spots_ref, *refs):
        x_refs = refs[:n_in] if n_in > 1 else [refs[0].at[i] for i in range(NX)]
        w_refs = refs[n_in : n_in + n_w]
        pi_ref, po_ref = refs[n_in + n_w : n_in + n_w + 2]
        into_ref = refs[n_in + n_w + 2]
        refs = refs[n_in + n_w + 2 + len(extra) + len(after) :]
        out_ref, mark_ref, wg, wu, wd, xs, cs, sem = refs
        mark_ref[...] = jnp.zeros_like(mark_ref)
        if not one:
            out_ref[...] = jnp.zeros_like(out_ref) if into is None else into_ref[...]
        gate_w, up_w, down_w = w_refs[:3]

        def copies(f):
            span = pl.ds(f * chunk, chunk)
            return (
                pltpu.make_async_copy(gate_w.at[:, span], wg.at[f], sem.at[f, 0]),
                pltpu.make_async_copy(up_w.at[:, span], wu.at[f], sem.at[f, 1]),
                pltpu.make_async_copy(down_w.at[:, span], wd.at[f], sem.at[f, 2]),
            )

        for f in range(chunks):
            for c in copies(f):
                c.start()
        for k in range(NC):
            for i in range(NX):
                xs[k, i * main : (i + 1) * main, :] = x_refs[i][k, 0:main, :]
                cs[k, i * main : (i + 1) * main, :] = x_refs[i][k, main : 2 * main, :]
            spare = [x_refs[i][k, 2 * main : 2 * main + 8, :].astype(F32) for i in range(NX)]
            spare = jnp.concatenate(spare, axis=0).astype(BF)
            xs[k, base:, :] = spare
            cs[k, base:, :] = spare
        for k in reversed(range(NC)):
            inner, outer_ = None, None
            for f in range(chunks):
                span = slice(f * chunk, (f + 1) * chunk)
                if k:
                    gate_c, up_c, down_c = w_refs[3][:, span], w_refs[4][:, span], w_refs[5][:, span]
                else:
                    for c in copies(f):
                        c.wait()
                    gate_c, up_c, down_c = wg[f], wu[f], wd[f]
                x = xs[k]
                gate = jnp.dot(x, gate_c, preferred_element_type=F32)
                up = jnp.dot(x, up_c, preferred_element_type=F32)
                back = jnp.dot(cs[k], down_c, preferred_element_type=F32)
                tail = back[base:]
                tail = jnp.concatenate([tail[2 * n :], tail[: 2 * n]], axis=0)
                back = jnp.concatenate([back[:base], tail], axis=0)
                sig = jax.nn.sigmoid(gate)
                hidden = (gate * sig * up).astype(BF)
                delta = (back * up * sig * (1.0 + gate * (1.0 - sig))).astype(BF)
                hid = lax.dot_general(hidden, pi_ref[:, span], contract, preferred_element_type=F32)
                dlt = lax.dot_general(delta, po_ref[:, span], contract, preferred_element_type=F32)
                inner = hid if inner is None else inner + hid
                outer_ = dlt if outer_ is None else outer_ + dlt
            acc = jnp.concatenate([inner, outer_], axis=1)
            for i in range(NX):
                over = acc[base + 8 * i : base + 8 * i + 8]
                for a in range(n):
                    lo = i * main + a * MAIN
                    block = jnp.concatenate([acc[lo : lo + MAIN], over], axis=0).astype(BF)
                    to = spots_ref[i] if n_in > 1 else i
                    out_ref[to, 0 if one else spots_ref[NX + a], k] = block

    vmem = pl.BlockSpec(memory_space=pltpu.VMEM)
    return pl.pallas_call(
        kernel,
        name="expert",
        out_shape=[pltpu.VMEM((NX, 1 if one else NZ, NC, part, 2 * r), BF), MARK],
        in_specs=[pl.BlockSpec(memory_space=pltpu.SMEM)] + [vmem] * n_in + [pl.BlockSpec(memory_space=pltpu.HBM)] * 3 + [vmem] * (3 + 2 + len(extra) + len(after)),
        out_specs=[vmem] * 2,
        scratch_shapes=[
            pltpu.VMEM((chunks, d, chunk), BF),
            pltpu.VMEM((chunks, d, chunk), BF),
            pltpu.VMEM((chunks, d, chunk), BF),
            pltpu.VMEM((NC, m, d), BF),
            pltpu.VMEM((NC, m, d), BF),
            pltpu.SemaphoreType.DMA((chunks, 3)),
        ],
        compiler_params=pltpu.CompilerParams(vmem_limit_bytes=VMEM),
    )(spots, *recv, *in_hbm(weights[:3]), *in_vmem(weights[3:]), proj_in, proj_out, *in_vmem(extra), *in_vmem(after))


def features(tokens, cotangent, proj_in, proj_out):
    t = tokens.shape[0]
    r = proj_in.shape[0]
    contract = (((1,), (1,)), ((), ()))

    def kernel(x_ref, c_ref, pi_ref, po_ref, out_ref):
        out_ref[:, 0:r] = lax.dot_general(x_ref[...], pi_ref[...], contract, preferred_element_type=F32).astype(BF)
        out_ref[:, r:] = lax.dot_general(c_ref[...], po_ref[...], contract, preferred_element_type=F32).astype(BF)

    return pl.pallas_call(
        kernel,
        name="features",
        out_shape=pltpu.VMEM((t, 2 * r), BF),
        compiler_params=pltpu.CompilerParams(vmem_limit_bytes=VMEM),
    )(tokens, cotangent, proj_in, proj_out)


def outer(ids, back, place, routes_t, weight_t, example, table, into=None):
    r = table.shape[1] // 2
    part = MAIN + 8
    k = NJ * part
    half = r // 2

    def kernel(ids_ref, routes_ref, weight_ref, ex_ref, table_ref, *refs):
        back_ref, refs = refs[0], refs[1:]
        if into is None:
            out_ref = refs[0]
        else:
            final_ref, out_ref, sem = refs[1:]
        routes = routes_ref[...].astype(F32)
        weight = weight_ref[...]
        example = ex_ref[...].astype(F32)
        lane = lax.broadcasted_iota(I32, (1, 2 * r), 1)
        col = lax.broadcasted_iota(I32, (k, NJ * 2 * r), 1) // (2 * r)
        row = lax.broadcasted_iota(I32, (k, NJ * 2 * r), 0) // part
        own = col == row
        pr = lax.broadcasted_iota(I32, (part, 1), 0)
        for p, shard in enumerate(place):
            eid = [ids_ref[p * NJ + j] for j in range(NJ)]
            keys = expert_keys(routes, [e.astype(F32) for e in eid])
            q = pr - MAIN - shard * SPARE
            slots = jnp.where(pr < MAIN, pr, jnp.where((q >= 0) & (q < SPARE), MAIN + q, -9)).astype(F32)
            hot, scale, held, second = [], [], [], []
            for j in range(NJ):
                h = jnp.where(keys[j : j + 1] == slots, 1.0, 0.0)
                we = jnp.sum(jnp.where(routes == eid[j].astype(F32), weight, 0.0), axis=0, keepdims=True)
                hot.append(h)
                scale.append(jnp.sum(h * we, axis=1, keepdims=True))
                held.append(jnp.sum(h, axis=1, keepdims=True))
                second.append(jnp.sum(h * example, axis=1, keepdims=True))
            hot = jnp.concatenate(hot, axis=0).astype(BF)
            scale = jnp.concatenate(scale, axis=0)
            held = jnp.concatenate(held, axis=0)
            second = jnp.concatenate(second, axis=0)
            mem = jnp.where(lane < r, held - second, second)
            sel = jnp.dot(hot, table_ref[...], preferred_element_type=F32) * scale
            if into is None:
                at = ids_ref[len(place) * NJ + p]
                got = [back_ref[j // NC * NZ + at, j % NC].astype(F32) for j in range(NJ)]
            else:
                got = [back_ref[j // NC, j % NC].astype(F32) for j in range(NJ)]
            got = jnp.concatenate(got, axis=0)
            twice = lambda v: jnp.concatenate([v, v], axis=1)
            im = twice(sel[:, 0:r]) * mem
            om = twice(sel[:, r:])
            inner = twice(got[:, 0:r]) * mem
            outh = twice(got[:, r:])
            for g, (left, right) in enumerate(((im, outh), (inner, om))):
                wide = jnp.concatenate([right] * NJ, axis=1)
                wide = jnp.where(own, wide, 0.0).astype(BF)
                res = lax.dot_general(
                    left.astype(BF), wide, (((0,), (0,)), ((), ())), preferred_element_type=F32
                )
                for j in range(NJ):
                    for s in range(EX_DEV):
                        even = res[s * r : s * r + half, j * 2 * r : (j + 1) * 2 * r]
                        odd = res[s * r + half : (s + 1) * r, j * 2 * r : (j + 1) * 2 * r]
                        block = jnp.where(lane < r, even, odd).astype(BF)
                        if into is None:
                            out_ref[s, eid[j], g] = block
                        else:
                            out_ref[s, j, g] = block
            if into is not None:
                copies = []
                for s in range(EX_DEV):
                    for j in range(NJ):
                        dst = final_ref.at[s, eid[j]]
                        copies.append(pltpu.make_async_copy(out_ref.at[s, j], dst, sem.at[s * NJ + j]))
                for c in copies:
                    c.start()
                for c in copies:
                    c.wait()

    vmem = pl.BlockSpec(memory_space=pltpu.VMEM)
    extra, out_specs, scratch, alias = [], vmem, [], {}
    if into is not None:
        assert len(place) == 1
        extra, out_specs = [into], pl.BlockSpec(memory_space=pl.ANY)
        scratch = [pltpu.VMEM((EX_DEV, NJ, 2, half, 2 * r), BF), pltpu.SemaphoreType.DMA((EX_DEV * NJ,))]
        alias = {6: 0}
    return pl.pallas_call(
        kernel,
        name="outer",
        out_shape=jax.ShapeDtypeStruct((EX_DEV, NZ * NJ, 2, half, 2 * r), BF),
        in_specs=[pl.BlockSpec(memory_space=pltpu.SMEM)]
        + [vmem] * 5
        + [pl.BlockSpec(memory_space=pl.ANY)] * len(extra),
        out_specs=out_specs,
        scratch_shapes=scratch,
        input_output_aliases=alias,
        compiler_params=pltpu.CompilerParams(vmem_limit_bytes=VMEM),
    )(ids, routes_t, weight_t, example, table, back, *extra)


def ordered(arrays, after):
    whole, vmem = pl.BlockSpec(memory_space=pltpu.HBM), pl.BlockSpec(memory_space=pltpu.VMEM)

    def kernel(*refs):
        refs[-1][...] = jnp.zeros_like(refs[-1])

    return pl.pallas_call(
        kernel,
        name="ordered",
        out_shape=[pltpu.HBM(a.shape, a.dtype) for a in arrays] + [MARK],
        in_specs=[whole] * len(arrays) + [vmem] * len(after),
        out_specs=[whole] * len(arrays) + [vmem],
        input_output_aliases={i: i for i in range(len(arrays))},
    )(*in_hbm(arrays), *in_vmem(after))


def pause(after):
    vmem = pl.BlockSpec(memory_space=pltpu.VMEM)

    def kernel(*refs):
        refs[-1][...] = jnp.zeros_like(refs[-1])

    return pl.pallas_call(
        kernel,
        name="pause",
        cost_estimate=LONG,
        out_shape=MARK,
        in_specs=[vmem] * len(after),
        out_specs=vmem,
    )(*in_vmem(after))


def along_z(a, k):
    return lax.ppermute(a, "z", [(i, (i + k) % NZ) for i in range(NZ)])


def along_x(a, k):
    return a if k == 0 else lax.ppermute(a, "x", [(i, (i + k) % NX) for i in range(NX)])


def partner(a):
    return lax.ppermute(a, "c", [(0, 1), (1, 0)])


def shards(
    tokens, cotangent, routes, route_weight, example_ids, w_gate, w_up, w_down, proj_model, proj_hidden
):
    tok_dev, d = tokens.shape
    r = proj_model.shape[0]
    x, z, c = (lax.axis_index(axis) for axis in ("x", "z", "c"))
    plane = lambda zz: jnp.stack(
        [(x + k) % NX * (NZ * NC) + zz * NC + (c ^ other) for k in STEPS_X for other in range(NC)]
    )
    here = jnp.concatenate([plane(z), jnp.stack([(x + k) % NX for k in STEPS_X])])

    routes_t = routes.T
    weight_t = route_weight.T
    extra = jnp.pad(routes_t.astype(BF), ((0, 8), (0, d - tok_dev)))
    own = jnp.concatenate([tokens, cotangent, extra], axis=0)

    order = lambda p: jnp.concatenate([p[0::2], p[1::2]], axis=0)
    proj_in, proj_out = order(proj_hidden), proj_hidden
    weights = [w_gate[0], w_up[0], w_down[0].T]
    weights = weights + [partner(w) for w in weights]
    table = features(tokens, cotangent, order(proj_model), proj_model)
    sources = [(x - k) % NX for k in STEPS_X]

    recvs, marks, most = [], [], None
    places = [[0], [-1, 1], [-2, 2], [-3, 3], [4]]

    def run_expert(i, into, after):
        spots = jnp.stack(sources + [(z + k) % NZ for k in places[i]])
        return expert(spots, recvs[i], len(places[i]), weights, proj_in, proj_out, into, after)

    for i, dist in enumerate(places):
        refs = [own]
        if i == 0:
            ahead, gap = [along_z(own, 1), along_z(own, -1)], [pause([])]
        elif i < 4:
            *refs, mark = ordered(ahead, [table, mark] if i == 1 else [mark, marks[i - 2]])
            gap = [pause([mark])]
            ahead = [along_z(refs[0], 1), along_z(refs[1], -1)] if i < 3 else [along_z(refs[0], 1)]
        else:
            refs, gap = ahead, []
        joined = i in JOINED
        *sent, mark = dispatch(refs, here, tok_dev, joined, gap + (marks[i - 2 : i - 1] if i >= 2 else []))
        if joined:
            recvs.append([lax.all_to_all(sent[0], "x", split_axis=0, concat_axis=0, tiled=True)])
        else:
            recvs.append([along_x(a, k) for a, k in zip(sent, STEPS_X)])
        if i:
            most, done = run_expert(i - 1, most, [mark if i < 4 else pause([mark])])
            marks.append(done)

    shape = most.shape[2:]
    most = most.reshape((NX * NZ,) + shape)
    most = lax.all_to_all(most, ("x", "z"), split_axis=0, concat_axis=0, tiled=True)
    last, _ = run_expert(4, False, [pause(recvs[4][1:])])
    last = along_z(last.reshape((NX,) + shape), 4)
    last = lax.all_to_all(last, "x", split_axis=0, concat_axis=0, tiled=True)

    j = jnp.arange(NJ, dtype=I32)
    fixed = lambda zz: (j // NC) * (NZ * NC) + zz * NC + (c ^ (j % NC))
    near = [(k, a) for dist in places[:-1] for a, k in enumerate(dist)]
    planes = [(z - k) % NZ for k, _ in near]
    ids = jnp.concatenate([fixed(p) for p in planes] + [jnp.stack(planes)])
    mine = (routes_t, weight_t, example_ids[None, :], table)
    out = outer(ids, most, [a for _, a in near], *mine)
    out = outer(fixed((z + 4) % NZ), last, [0], *mine, into=out)
    return out.reshape(EX_DEV, NZ * NJ, 2, r * r)


def solution(mesh):
    dp = mesh.shape["dp"]
    torus = Mesh(mesh.devices.reshape(dp, NX, NZ, NC), ("dp", "x", "z", "c"))
    part, ex = ("dp", "x", "z", "c"), ("x", "z", "c")
    placed = (
        P(part, None),
        P(part, None),
        P(part, None),
        P(part, None),
        P(part),
        P(ex, None, None),
        P(ex, None, None),
        P(ex, None, None),
        P(),
        P(),
    )
    return jax.shard_map(
        shards, mesh=torus, in_specs=placed, out_specs=P(part, None, None, None), check_vma=False
    )
```

```python
import jax
import jax.numpy as jnp
from jax import lax
from jax.experimental import pallas as pl
from jax.experimental.pallas import tpu as pltpu
from jax.sharding import Mesh
from jax.sharding import PartitionSpec as P

NX, NZ, NC = 4, 8, 2
NJ = NX * NC
STEPS_X = (0, 1, 3, 2)
JOINED = (0, 2)
CAP, MAIN = 18, 16
SPARE = CAP - MAIN
EX_DEV = 2
BF, F32, I32 = jnp.bfloat16, jnp.float32, jnp.int32
VMEM = 24 * 1024 * 1024
MARK = pltpu.VMEM((8, 128), F32)
LONG = pl.CostEstimate(flops=int(4e10), bytes_accessed=int(12e6), transcendentals=0)


def in_hbm(arrays):
    return [pltpu.with_memory_space_constraint(a, pltpu.HBM) for a in arrays]


def in_vmem(arrays):
    return [pltpu.with_memory_space_constraint(a, pltpu.VMEM) for a in arrays]


def block_rows(n):
    return 2 * n * MAIN + 8


def row_slots(n, shard, array, offset_rows=0):
    r = lax.broadcasted_iota(I32, (block_rows(n), 1), 0)
    main = n * MAIN
    base = array * main + shard * MAIN
    spare = 2 * main + array * SPARE * n + shard * SPARE
    slot = jnp.where((r >= base) & (r < base + MAIN), r - base, -9)
    return jnp.where((r >= spare) & (r < spare + SPARE), MAIN + r - spare, slot)


def expert_keys(routes, ids):
    masks = [jnp.max(jnp.where(routes == e, 1.0, 0.0), axis=0, keepdims=True) for e in ids]
    mask = jnp.concatenate(masks, axis=0)
    t = mask.shape[1]
    before = lax.broadcasted_iota(I32, (t, t), 0) < lax.broadcasted_iota(I32, (t, t), 1)
    tri = jnp.where(before, 1.0, 0.0).astype(BF)
    rank = jnp.dot(mask.astype(BF), tri, preferred_element_type=F32)
    return jnp.where(mask > 0, rank, -1.0)


def assemble(tokens, cotangent, routes):
    t, d = tokens.shape

    parts = 4
    size = 2 * t // parts

    def kernel(x_ref, c_ref, routes_ref, out_ref, held, sem):
        def rows(i):
            return pl.ds(i * size, size)

        def copy_in(i):
            ref, at = (x_ref, i) if i < parts // 2 else (c_ref, i - parts // 2)
            return pltpu.make_async_copy(ref.at[rows(at)], held.at[rows(i)], sem.at[0, i])

        def copy_out(i):
            return pltpu.make_async_copy(held.at[rows(i)], out_ref.at[rows(i)], sem.at[1, i])

        for i in range(parts):
            copy_in(i).start()
        near = routes_ref[...].astype(F32)
        near = jnp.concatenate([near, jnp.zeros_like(near)], axis=0).astype(BF)
        held[2 * t :, :] = jnp.zeros((16, d), BF)
        held[2 * t :, 0:t] = near
        last = pl.ds(2 * t, 16)
        tail = pltpu.make_async_copy(held.at[last], out_ref.at[last], sem.at[0, parts])
        tail.start()
        for i in range(parts):
            copy_in(i).wait()
            copy_out(i).start()
        for i in range(parts):
            copy_out(i).wait()
        tail.wait()

    hbm = pl.BlockSpec(memory_space=pltpu.HBM)
    return pl.pallas_call(
        kernel,
        name="assemble",
        out_shape=pltpu.HBM((2 * t + 16, d), BF),
        in_specs=[hbm, hbm, pl.BlockSpec(memory_space=pltpu.VMEM)],
        out_specs=hbm,
        scratch_shapes=[pltpu.VMEM((2 * t + 16, d), BF), pltpu.SemaphoreType.DMA((2, parts + 1))],
    )(*in_hbm([tokens, cotangent]), routes)


def dispatch(shard_refs, ids, tok_dev, joined, after=()):
    n = len(shard_refs)
    rows = block_rows(n)
    d = shard_refs[0].shape[1]
    chunks = 4
    cols = d // chunks
    both = 2 * tok_dev
    n_out, lead = (1, (NX,)) if joined else (NX, ())

    def kernel(ids_ref, *refs):
        ins, refs = refs[:n], refs[n + len(after) :]
        outs, mark_ref = refs[:n_out], refs[n_out]
        held, sent, hot_ref, near, in_sem, out_sem, near_sem = refs[n_out + 1 :]

        def span(q):
            return pl.ds(q * cols, cols)

        def copy_in(i, q):
            src = ins[i].at[pl.ds(0, both), span(q)]
            return pltpu.make_async_copy(src, held.at[pl.ds(i * both, both), span(q)], in_sem.at[i, q])

        def copy_out(i, q):
            to = outs[0].at[ids_ref[NJ + i]] if joined else outs[i]
            src = sent.at[pl.ds(i * NC, NC), :, span(q)]
            return pltpu.make_async_copy(src, to.at[:, :, span(q)], out_sem.at[i, q])

        def copy_near(i):
            src = ins[i].at[pl.ds(both, 16), pl.ds(0, tok_dev)]
            return pltpu.make_async_copy(src, near.at[i], near_sem.at[i])

        for i in range(n):
            copy_near(i).start()
        for q in range(chunks):
            for i in range(n):
                copy_in(i, q).start()
        mark_ref[...] = jnp.zeros_like(mark_ref)
        eid = [ids_ref[j].astype(F32) for j in range(NJ)]
        for a in range(n):
            copy_near(a).wait()
            keys = expert_keys(near[a].astype(F32)[0:8], eid)
            for array in range(2):
                slots = row_slots(n, a, array).astype(F32)
                hot = [jnp.where(keys[j : j + 1] == slots, 1.0, 0.0) for j in range(NJ)]
                hot = jnp.concatenate(hot, axis=0).astype(BF)
                at = a * both + array * tok_dev
                hot_ref[:, at : at + tok_dev] = hot
        for q in range(chunks):
            for i in range(n):
                copy_in(i, q).wait()
            here = slice(q * cols, (q + 1) * cols)
            acc = jnp.dot(hot_ref[...], held[:, here], preferred_element_type=F32)
            for j in range(NJ):
                sent[j, :, here] = acc[j * rows : (j + 1) * rows].astype(BF)
            for i in range(NX):
                copy_out(i, q).start()
        for q in range(chunks):
            for i in range(NX):
                copy_out(i, q).wait()

    vmem, hbm = pl.BlockSpec(memory_space=pltpu.VMEM), pl.BlockSpec(memory_space=pltpu.HBM)
    return pl.pallas_call(
        kernel,
        name="dispatch",
        out_shape=[pltpu.HBM(lead + (NC, rows, d), BF)] * n_out + [MARK],
        in_specs=[pl.BlockSpec(memory_space=pltpu.SMEM)] + [hbm] * n + [vmem] * len(after),
        out_specs=[hbm] * n_out + [vmem],
        scratch_shapes=[
            pltpu.VMEM((n * both, d), BF),
            pltpu.VMEM((NJ, rows, d), BF),
            pltpu.VMEM((NJ * rows, n * both), BF),
            pltpu.VMEM((n, 16, tok_dev), BF),
            pltpu.SemaphoreType.DMA((n, chunks)),
            pltpu.SemaphoreType.DMA((NX, chunks)),
            pltpu.SemaphoreType.DMA((n,)),
        ],
        compiler_params=pltpu.CompilerParams(vmem_limit_bytes=VMEM),
    )(ids, *in_hbm(shard_refs), *in_vmem(after))


def expert(spots, recv, n, weights, proj_in, proj_out, into, after=()):
    rows, d = recv[0].shape[-2:]
    n_in = len(recv)
    ff = weights[0].shape[-1]
    r = proj_in.shape[0]
    chunk = 256
    chunks = ff // chunk
    n_w = len(weights)
    main = n * MAIN
    base = NX * main
    m = base + NX * 8
    part = MAIN + 8
    contract = (((1,), (1,)), ((), ()))

    extra = [] if into is None else [into]

    def kernel(spots_ref, *refs):
        x_refs = list(refs[:n_in]) if n_in > 1 else [refs[0].at[i] for i in range(NX)]
        w_refs = refs[n_in : n_in + n_w]
        pi_ref, po_ref = refs[n_in + n_w : n_in + n_w + 2]
        refs = refs[n_in + n_w + 2 + len(extra) + len(after) :]
        out_ref, mark_ref, wg, wu, wd, xs, cs, done, held, sem, out_sem, own_sem = refs
        if n_in > 1:
            own = pltpu.make_async_copy(x_refs[0], held, own_sem)
            own.start()
            x_refs[0] = held
        mark_ref[...] = jnp.zeros_like(mark_ref)
        gate_w, up_w, down_w = w_refs[:3]

        def copies(f):
            span = pl.ds(f * chunk, chunk)
            return (
                pltpu.make_async_copy(gate_w.at[:, span], wg.at[f], sem.at[f, 0]),
                pltpu.make_async_copy(up_w.at[:, span], wu.at[f], sem.at[f, 1]),
                pltpu.make_async_copy(down_w.at[:, span], wd.at[f], sem.at[f, 2]),
            )

        for c in copies(0):
            c.start()
        for i in reversed(range(NX)):
            if i == 0 and n_in > 1:
                own.wait()
            for k in range(NC):
                xs[k, i * main : (i + 1) * main, :] = x_refs[i][k, 0:main, :]
                cs[k, i * main : (i + 1) * main, :] = x_refs[i][k, main : 2 * main, :]
        for f in range(1, chunks):
            for c in copies(f):
                c.start()
        for k in range(NC):
            spare = [x_refs[i][k, 2 * main : 2 * main + 8, :].astype(F32) for i in range(NX)]
            spare = jnp.concatenate(spare, axis=0).astype(BF)
            xs[k, base:, :] = spare
            cs[k, base:, :] = spare
        home = []
        for k in reversed(range(NC)):
            inner, outer_ = None, None
            for f in range(1 if k else chunks):
                span = slice(0, ff) if k else slice(f * chunk, (f + 1) * chunk)
                if k:
                    gate_c, up_c, down_c = w_refs[3][:, span], w_refs[4][:, span], w_refs[5][:, span]
                else:
                    for c in copies(f):
                        c.wait()
                    gate_c, up_c, down_c = wg[f], wu[f], wd[f]
                x = xs[k]
                gate = jnp.dot(x, gate_c, preferred_element_type=F32)
                up = jnp.dot(x, up_c, preferred_element_type=F32)
                back = jnp.dot(cs[k], down_c, preferred_element_type=F32)
                tail = back[base:]
                tail = jnp.concatenate([tail[2 * n :], tail[: 2 * n]], axis=0)
                back = jnp.concatenate([back[:base], tail], axis=0)
                sig = jax.nn.sigmoid(gate)
                hidden = (gate * sig * up).astype(BF)
                delta = (back * up * sig * (1.0 + gate * (1.0 - sig))).astype(BF)
                hid = lax.dot_general(hidden, pi_ref[:, span], contract, preferred_element_type=F32)
                dlt = lax.dot_general(delta, po_ref[:, span], contract, preferred_element_type=F32)
                inner = hid if inner is None else inner + hid
                outer_ = dlt if outer_ is None else outer_ + dlt
            acc = jnp.concatenate([inner, outer_], axis=1)
            for i in range(NX):
                over = acc[base + 8 * i : base + 8 * i + 8]
                for a in range(n):
                    lo = i * main + a * MAIN
                    block = jnp.concatenate([acc[lo : lo + MAIN], over], axis=0).astype(BF)
                    done[a, i, k] = block
                    to = out_ref.at[spots_ref[i] if n_in > 1 else i, spots_ref[NX + a], k]
                    home.append(pltpu.make_async_copy(done.at[a, i, k], to, out_sem.at[a, i, k]))
                    home[-1].start()
        for c in home:
            c.wait()

    vmem, hbm = pl.BlockSpec(memory_space=pltpu.VMEM), pl.BlockSpec(memory_space=pltpu.HBM)
    return pl.pallas_call(
        kernel,
        name="expert",
        out_shape=[pltpu.HBM((NX, NZ, NC, part, 2 * r), BF), MARK],
        in_specs=[pl.BlockSpec(memory_space=pltpu.SMEM)]
        + [hbm if n_in > 1 else vmem]
        + [vmem] * (n_in - 1)
        + [hbm] * 3
        + [vmem] * 5
        + [hbm] * len(extra)
        + [vmem] * len(after),
        out_specs=[hbm, vmem],
        input_output_aliases={1 + n_in + n_w + 2: 0} if extra else {},
        scratch_shapes=[
            pltpu.VMEM((chunks, d, chunk), BF),
            pltpu.VMEM((chunks, d, chunk), BF),
            pltpu.VMEM((chunks, d, chunk), BF),
            pltpu.VMEM((NC, m, d), BF),
            pltpu.VMEM((NC, m, d), BF),
            pltpu.VMEM((n, NX, NC, part, 2 * r), BF),
            pltpu.VMEM((NC, rows, d), BF),
            pltpu.SemaphoreType.DMA((chunks, 3)),
            pltpu.SemaphoreType.DMA((n, NX, NC)),
            pltpu.SemaphoreType.DMA,
        ],
        compiler_params=pltpu.CompilerParams(vmem_limit_bytes=VMEM),
    )(spots, *(in_hbm(recv[:1]) + recv[1:] if n_in > 1 else recv), *in_hbm(weights[:3]), *in_vmem(weights[3:]), proj_in, proj_out, *in_hbm(extra), *in_vmem(after))


def features(tokens, cotangent, proj_in, proj_out):
    t = tokens.shape[0]
    r = proj_in.shape[0]
    contract = (((1,), (1,)), ((), ()))

    def kernel(x_ref, c_ref, pi_ref, po_ref, out_ref):
        out_ref[:, 0:r] = lax.dot_general(x_ref[...], pi_ref[...], contract, preferred_element_type=F32).astype(BF)
        out_ref[:, r:] = lax.dot_general(c_ref[...], po_ref[...], contract, preferred_element_type=F32).astype(BF)

    return pl.pallas_call(
        kernel,
        name="features",
        out_shape=pltpu.VMEM((t, 2 * r), BF),
        compiler_params=pltpu.CompilerParams(vmem_limit_bytes=VMEM),
    )(tokens, cotangent, proj_in, proj_out)


def outer(ids, back, place, routes_t, weight_t, example, table, into=None):
    r = table.shape[1] // 2
    part = MAIN + 8
    k = NJ * part
    half = r // 2

    def kernel(ids_ref, routes_ref, weight_ref, ex_ref, table_ref, *refs):
        back_ref, refs = refs[0], refs[1:]
        if into is None:
            out_ref = refs[0]
        else:
            final_ref, out_ref, sem = refs[1:]
        routes = routes_ref[...].astype(F32)
        weight = weight_ref[...]
        example = ex_ref[...].astype(F32)
        lane = lax.broadcasted_iota(I32, (1, 2 * r), 1)
        col = lax.broadcasted_iota(I32, (k, NJ * 2 * r), 1) // (2 * r)
        row = lax.broadcasted_iota(I32, (k, NJ * 2 * r), 0) // part
        own = col == row
        pr = lax.broadcasted_iota(I32, (part, 1), 0)
        copies = []
        for p, shard in enumerate(place):
            eid = [ids_ref[p * NJ + j] for j in range(NJ)]
            keys = expert_keys(routes, [e.astype(F32) for e in eid])
            q = pr - MAIN - shard * SPARE
            slots = jnp.where(pr < MAIN, pr, jnp.where((q >= 0) & (q < SPARE), MAIN + q, -9)).astype(F32)
            hot, scale, held, second = [], [], [], []
            for j in range(NJ):
                h = jnp.where(keys[j : j + 1] == slots, 1.0, 0.0)
                we = jnp.sum(jnp.where(routes == eid[j].astype(F32), weight, 0.0), axis=0, keepdims=True)
                hot.append(h)
                scale.append(jnp.sum(h * we, axis=1, keepdims=True))
                held.append(jnp.sum(h, axis=1, keepdims=True))
                second.append(jnp.sum(h * example, axis=1, keepdims=True))
            hot = jnp.concatenate(hot, axis=0).astype(BF)
            scale = jnp.concatenate(scale, axis=0)
            held = jnp.concatenate(held, axis=0)
            second = jnp.concatenate(second, axis=0)
            mem = jnp.where(lane < r, held - second, second)
            sel = jnp.dot(hot, table_ref[...], preferred_element_type=F32) * scale
            at = ids_ref[len(place) * NJ + p]
            got = [back_ref[j // NC * NZ + at, j % NC].astype(F32) for j in range(NJ)]
            got = jnp.concatenate(got, axis=0)
            twice = lambda v: jnp.concatenate([v, v], axis=1)
            im = twice(sel[:, 0:r]) * mem
            om = twice(sel[:, r:])
            inner = twice(got[:, 0:r]) * mem
            outh = twice(got[:, r:])
            for g, (left, right) in enumerate(((im, outh), (inner, om))):
                wide = jnp.concatenate([right] * NJ, axis=1)
                wide = jnp.where(own, wide, 0.0).astype(BF)
                res = lax.dot_general(
                    left.astype(BF), wide, (((0,), (0,)), ((), ())), preferred_element_type=F32
                )
                for j in range(NJ):
                    for s in range(EX_DEV):
                        even = res[s * r : s * r + half, j * 2 * r : (j + 1) * 2 * r]
                        odd = res[s * r + half : (s + 1) * r, j * 2 * r : (j + 1) * 2 * r]
                        block = jnp.where(lane < r, even, odd).astype(BF)
                        if into is None:
                            out_ref[s, eid[j], g] = block
                        else:
                            out_ref[p, s, j, g] = block
            if into is not None:
                for s in range(EX_DEV):
                    for j in range(NJ):
                        to, i = final_ref.at[s, eid[j]], (p * EX_DEV + s) * NJ + j
                        copies.append(pltpu.make_async_copy(out_ref.at[p, s, j], to, sem.at[i]))
                        copies[-1].start()
        for c in copies:
            c.wait()

    vmem = pl.BlockSpec(memory_space=pltpu.VMEM)
    extra, out_specs, scratch, alias = [], vmem, [], {}
    if into is not None:
        extra, out_specs = [into], pl.BlockSpec(memory_space=pl.ANY)
        scratch = [
            pltpu.VMEM((len(place), EX_DEV, NJ, 2, half, 2 * r), BF),
            pltpu.SemaphoreType.DMA((len(place) * EX_DEV * NJ,)),
        ]
        alias = {6: 0}
    return pl.pallas_call(
        kernel,
        name="outer",
        out_shape=jax.ShapeDtypeStruct((EX_DEV, NZ * NJ, 2, half, 2 * r), BF),
        in_specs=[pl.BlockSpec(memory_space=pltpu.SMEM)]
        + [vmem] * 5
        + [pl.BlockSpec(memory_space=pl.ANY)] * len(extra),
        out_specs=out_specs,
        scratch_shapes=scratch,
        input_output_aliases=alias,
        compiler_params=pltpu.CompilerParams(vmem_limit_bytes=VMEM),
    )(ids, routes_t, weight_t, example, table, back, *extra)


def ordered(arrays, after):
    whole, vmem = pl.BlockSpec(memory_space=pltpu.HBM), pl.BlockSpec(memory_space=pltpu.VMEM)

    def kernel(*refs):
        refs[-1][...] = jnp.zeros_like(refs[-1])

    return pl.pallas_call(
        kernel,
        name="ordered",
        out_shape=[pltpu.HBM(a.shape, a.dtype) for a in arrays] + [MARK],
        in_specs=[whole] * len(arrays) + [vmem] * len(after),
        out_specs=[whole] * len(arrays) + [vmem],
        input_output_aliases={i: i for i in range(len(arrays))},
    )(*in_hbm(arrays), *in_vmem(after))


def pause(after):
    vmem = pl.BlockSpec(memory_space=pltpu.VMEM)

    def kernel(*refs):
        refs[-1][...] = jnp.zeros_like(refs[-1])

    return pl.pallas_call(
        kernel,
        name="pause",
        cost_estimate=LONG,
        out_shape=MARK,
        in_specs=[vmem] * len(after),
        out_specs=vmem,
    )(*in_vmem(after))


def along_z(a, k):
    return lax.ppermute(a, "z", [(i, (i + k) % NZ) for i in range(NZ)])


def along_x(a, k):
    return a if k == 0 else lax.ppermute(a, "x", [(i, (i + k) % NX) for i in range(NX)])


def partner(a):
    return lax.ppermute(a, "c", [(0, 1), (1, 0)])


def shards(
    tokens, cotangent, routes, route_weight, example_ids, w_gate, w_up, w_down, proj_model, proj_hidden
):
    tok_dev, d = tokens.shape
    r = proj_model.shape[0]
    x, z, c = (lax.axis_index(axis) for axis in ("x", "z", "c"))
    plane = lambda zz: jnp.stack(
        [(x + k) % NX * (NZ * NC) + zz * NC + (c ^ other) for k in STEPS_X for other in range(NC)]
    )
    here = jnp.concatenate([plane(z), jnp.stack([(x + k) % NX for k in STEPS_X])])

    routes_t = routes.T
    weight_t = route_weight.T
    own = assemble(tokens, cotangent, routes_t)

    order = lambda p: jnp.concatenate([p[0::2], p[1::2]], axis=0)
    proj_in, proj_out = order(proj_hidden), proj_hidden
    weights = [w_gate[0], w_up[0], w_down[0].T]
    weights = weights + [partner(w) for w in weights]
    table = features(tokens, cotangent, order(proj_model), proj_model)
    sources = [(x - k) % NX for k in STEPS_X]

    recvs, marks, back = [], [], None
    places = [[0], [-1, 1], [-2, 2], [-3, 3], [4]]

    def run_expert(i, into, after):
        spots = jnp.stack(sources + [(z + k) % NZ for k in places[i]])
        return expert(spots, recvs[i], len(places[i]), weights, proj_in, proj_out, into, after)

    for i, dist in enumerate(places):
        refs = [own]
        if i == 0:
            ahead, gap = [along_z(own, 1), along_z(own, -1)], [pause([])]
        elif i < 4:
            *refs, mark = ordered(ahead, [table, mark] if i == 1 else [mark, marks[i - 2]])
            gap = [pause([mark])]
            ahead = [along_z(refs[0], 1), along_z(refs[1], -1)] if i < 3 else [along_z(refs[0], 1)]
        else:
            refs, gap = ahead, []
        joined = i in JOINED
        *sent, mark = dispatch(refs, here, tok_dev, joined, gap + (marks[i - 2 : i - 1] if i >= 2 else []))
        if joined:
            recvs.append([lax.all_to_all(sent[0], "x", split_axis=0, concat_axis=0, tiled=True)])
        else:
            recvs.append([along_x(a, k) for a, k in zip(sent, STEPS_X)])
        if i:
            if i == 4:
                first, back = back, None
            back, done = run_expert(i - 1, back, [mark if i < 4 else pause([mark])])
            marks.append(done)

    back, _ = run_expert(4, back, [])

    def home(a):
        a = a.reshape((NX * NZ,) + a.shape[2:])
        return lax.all_to_all(a, ("x", "z"), split_axis=0, concat_axis=0, tiled=True)

    j = jnp.arange(NJ, dtype=I32)
    fixed = lambda zz: (j // NC) * (NZ * NC) + zz * NC + (c ^ (j % NC))
    mine = (routes_t, weight_t, example_ids[None, :], table)
    out = None
    for a, steps in ((first, places[:3]), (back, places[3:])):
        near = [(k, shard) for dist in steps for shard, k in enumerate(dist)]
        planes = [(z - k) % NZ for k, _ in near]
        ids = jnp.concatenate([fixed(p) for p in planes] + [jnp.stack(planes)])
        out = outer(ids, home(a), [shard for _, shard in near], *mine, into=out)
    return out.reshape(EX_DEV, NZ * NJ, 2, r * r)


def solution(mesh):
    dp = mesh.shape["dp"]
    torus = Mesh(mesh.devices.reshape(dp, NX, NZ, NC), ("dp", "x", "z", "c"))
    part, ex = ("dp", "x", "z", "c"), ("x", "z", "c")
    placed = (
        P(part, None),
        P(part, None),
        P(part, None),
        P(part, None),
        P(part),
        P(ex, None, None),
        P(ex, None, None),
        P(ex, None, None),
        P(),
        P(),
    )
    return jax.shard_map(
        shards, mesh=torus, in_specs=placed, out_specs=P(part, None, None, None), check_vma=False
    )
```

```python
import jax
import jax.numpy as jnp
from jax import lax
from jax.experimental import pallas as pl
from jax.experimental.pallas import tpu as pltpu
from jax.sharding import Mesh
from jax.sharding import PartitionSpec as P

NX, NZ, NC = 4, 8, 2
NJ = NX * NC
STEPS_X = (0, 1, 3, 2)
JOINED = (0, 2)
CAP, MAIN = 18, 16
SPARE = CAP - MAIN
EX_DEV = 2
BF, F32, I32 = jnp.bfloat16, jnp.float32, jnp.int32
VMEM = 24 * 1024 * 1024
MARK = pltpu.VMEM((8, 128), F32)
LONG = pl.CostEstimate(flops=int(4e10), bytes_accessed=int(12e6), transcendentals=0)


def in_hbm(arrays):
    return [pltpu.with_memory_space_constraint(a, pltpu.HBM) for a in arrays]


def in_vmem(arrays):
    return [pltpu.with_memory_space_constraint(a, pltpu.VMEM) for a in arrays]


def block_rows(n):
    return 2 * n * MAIN + 8


def row_slots(n, shard, array):
    r = lax.broadcasted_iota(I32, (n * MAIN + 8, 1), 0)
    base = shard * MAIN
    spare = n * MAIN + array * SPARE * n + shard * SPARE
    slot = jnp.where((r >= base) & (r < base + MAIN), r - base, -9)
    return jnp.where((r >= spare) & (r < spare + SPARE), MAIN + r - spare, slot)


def expert_keys(routes, ids):
    masks = [jnp.max(jnp.where(routes == e, 1.0, 0.0), axis=0, keepdims=True) for e in ids]
    mask = jnp.concatenate(masks, axis=0)
    t = mask.shape[1]
    before = lax.broadcasted_iota(I32, (t, t), 0) < lax.broadcasted_iota(I32, (t, t), 1)
    tri = jnp.where(before, 1.0, 0.0).astype(BF)
    rank = jnp.dot(mask.astype(BF), tri, preferred_element_type=F32)
    return jnp.where(mask > 0, rank, -1.0)


def assemble(tokens, cotangent, routes):
    t, d = tokens.shape

    parts = 4
    size = 2 * t // parts

    def kernel(x_ref, c_ref, routes_ref, out_ref, held, sem):
        def rows(i):
            return pl.ds(i * size, size)

        def copy_in(i):
            ref, at = (x_ref, i) if i < parts // 2 else (c_ref, i - parts // 2)
            return pltpu.make_async_copy(ref.at[rows(at)], held.at[rows(i)], sem.at[0, i])

        def copy_out(i):
            return pltpu.make_async_copy(held.at[rows(i)], out_ref.at[rows(i)], sem.at[1, i])

        for i in range(parts):
            copy_in(i).start()
        near = routes_ref[...].astype(F32)
        near = jnp.concatenate([near, jnp.zeros_like(near)], axis=0).astype(BF)
        held[2 * t :, :] = jnp.zeros((16, d), BF)
        held[2 * t :, 0:t] = near
        last = pl.ds(2 * t, 16)
        tail = pltpu.make_async_copy(held.at[last], out_ref.at[last], sem.at[0, parts])
        tail.start()
        for i in range(parts):
            copy_in(i).wait()
            copy_out(i).start()
        for i in range(parts):
            copy_out(i).wait()
        tail.wait()

    hbm = pl.BlockSpec(memory_space=pltpu.HBM)
    return pl.pallas_call(
        kernel,
        name="assemble",
        out_shape=pltpu.HBM((2 * t + 16, d), BF),
        in_specs=[hbm, hbm, pl.BlockSpec(memory_space=pltpu.VMEM)],
        out_specs=hbm,
        scratch_shapes=[pltpu.VMEM((2 * t + 16, d), BF), pltpu.SemaphoreType.DMA((2, parts + 1))],
    )(*in_hbm([tokens, cotangent]), routes)


def dispatch(shard_refs, ids, tok_dev, joined, after=()):
    n = len(shard_refs)
    rows = block_rows(n)
    d = shard_refs[0].shape[1]
    chunks = 4
    cols = d // chunks
    both = 2 * tok_dev
    main = n * MAIN
    n_out, lead = (1, (NX,)) if joined else (NX, ())

    def kernel(ids_ref, *refs):
        ins, refs = refs[:n], refs[n + len(after) :]
        outs, mark_ref = refs[:n_out], refs[n_out]
        held, sent, hot_ref, near, in_sem, out_sem, near_sem = refs[n_out + 1 :]

        def span(q):
            return pl.ds(q * cols, cols)

        def copies_in(q):
            return [
                pltpu.make_async_copy(
                    ins[i].at[pl.ds(array * tok_dev, tok_dev), span(q)],
                    held.at[array, pl.ds(i * tok_dev, tok_dev), span(q)],
                    in_sem.at[i, q, array],
                )
                for i in range(n)
                for array in range(2)
            ]

        def copy_out(i, q):
            to = outs[0].at[ids_ref[NJ + i]] if joined else outs[i]
            src = sent.at[pl.ds(i * NC, NC), :, span(q)]
            return pltpu.make_async_copy(src, to.at[:, :, span(q)], out_sem.at[i, q])

        def copy_near(i):
            src = ins[i].at[pl.ds(both, 16), pl.ds(0, tok_dev)]
            return pltpu.make_async_copy(src, near.at[i], near_sem.at[i])

        for i in range(n):
            copy_near(i).start()
        for q in range(chunks):
            for c in copies_in(q):
                c.start()
        mark_ref[...] = jnp.zeros_like(mark_ref)
        eid = [ids_ref[j].astype(F32) for j in range(NJ)]
        for a in range(n):
            copy_near(a).wait()
            keys = expert_keys(near[a].astype(F32)[0:8], eid)
            for array in range(2):
                slots = row_slots(n, a, array).astype(F32)
                hot = [jnp.where(keys[j : j + 1] == slots, 1.0, 0.0) for j in range(NJ)]
                hot = jnp.concatenate(hot, axis=0).astype(BF)
                hot_ref[array, :, a * tok_dev : (a + 1) * tok_dev] = hot
        for q in range(chunks):
            for c in copies_in(q):
                c.wait()
            here = slice(q * cols, (q + 1) * cols)
            x, c = [jnp.dot(hot_ref[i], held[i, :, here], preferred_element_type=F32) for i in range(2)]
            for j in range(NJ):
                at = j * (main + 8)
                sent[j, 0:main, here] = x[at : at + main].astype(BF)
                sent[j, main : 2 * main, here] = c[at : at + main].astype(BF)
                at += main
                sent[j, 2 * main :, here] = (x[at : at + 8] + c[at : at + 8]).astype(BF)
            for i in range(NX):
                copy_out(i, q).start()
        for q in range(chunks):
            for i in range(NX):
                copy_out(i, q).wait()

    vmem, hbm = pl.BlockSpec(memory_space=pltpu.VMEM), pl.BlockSpec(memory_space=pltpu.HBM)
    return pl.pallas_call(
        kernel,
        name="dispatch",
        out_shape=[pltpu.HBM(lead + (NC, rows, d), BF)] * n_out + [MARK],
        in_specs=[pl.BlockSpec(memory_space=pltpu.SMEM)] + [hbm] * n + [vmem] * len(after),
        out_specs=[hbm] * n_out + [vmem],
        scratch_shapes=[
            pltpu.VMEM((2, n * tok_dev, d), BF),
            pltpu.VMEM((NJ, rows, d), BF),
            pltpu.VMEM((2, NJ * (main + 8), n * tok_dev), BF),
            pltpu.VMEM((n, 16, tok_dev), BF),
            pltpu.SemaphoreType.DMA((n, chunks, 2)),
            pltpu.SemaphoreType.DMA((NX, chunks)),
            pltpu.SemaphoreType.DMA((n,)),
        ],
        compiler_params=pltpu.CompilerParams(vmem_limit_bytes=VMEM),
    )(ids, *in_hbm(shard_refs), *in_vmem(after))


def expert(spots, recv, n, weights, proj_in, proj_out, into, after=()):
    rows, d = recv[0].shape[-2:]
    n_in = len(recv)
    ff = weights[0].shape[-1]
    r = proj_in.shape[0]
    chunk = 256
    chunks = ff // chunk
    n_w = len(weights)
    main = n * MAIN
    base = NX * main
    m = base + NX * 8
    part = MAIN + 8
    contract = (((1,), (1,)), ((), ()))

    extra = [] if into is None else [into]

    def kernel(spots_ref, *refs):
        x_refs = refs[:n_in] if n_in > 1 else [refs[0].at[i] for i in range(NX)]
        w_refs = refs[n_in : n_in + n_w]
        pi_ref, po_ref = refs[n_in + n_w : n_in + n_w + 2]
        refs = refs[n_in + n_w + 2 + len(extra) + len(after) :]
        out_ref, mark_ref, wg, wu, wd, xs, cs, done, sem, out_sem = refs
        mark_ref[...] = jnp.zeros_like(mark_ref)
        gate_w, up_w, down_w = w_refs[:3]

        def copies(f):
            span = pl.ds(f * chunk, chunk)
            return (
                pltpu.make_async_copy(gate_w.at[:, span], wg.at[f], sem.at[f, 0]),
                pltpu.make_async_copy(up_w.at[:, span], wu.at[f], sem.at[f, 1]),
                pltpu.make_async_copy(down_w.at[:, span], wd.at[f], sem.at[f, 2]),
            )

        for c in copies(0):
            c.start()
        for i in reversed(range(NX)):
            for k in range(NC):
                xs[k, i * main : (i + 1) * main, :] = x_refs[i][k, 0:main, :]
                cs[k, i * main : (i + 1) * main, :] = x_refs[i][k, main : 2 * main, :]
        for f in range(1, chunks):
            for c in copies(f):
                c.start()
        for k in range(NC):
            spare = [x_refs[i][k, 2 * main : 2 * main + 8, :].astype(F32) for i in range(NX)]
            spare = jnp.concatenate(spare, axis=0).astype(BF)
            xs[k, base:, :] = spare
            cs[k, base:, :] = spare
        home = []
        for k in reversed(range(NC)):
            inner, outer_ = None, None
            for f in range(1 if k else chunks):
                span = slice(0, ff) if k else slice(f * chunk, (f + 1) * chunk)
                if k:
                    gate_c, up_c, down_c = w_refs[3][:, span], w_refs[4][:, span], w_refs[5][:, span]
                else:
                    for c in copies(f):
                        c.wait()
                    gate_c, up_c, down_c = wg[f], wu[f], wd[f]
                x = xs[k]
                gate = jnp.dot(x, gate_c, preferred_element_type=F32)
                up = jnp.dot(x, up_c, preferred_element_type=F32)
                back = jnp.dot(cs[k], down_c, preferred_element_type=F32)
                tail = back[base:]
                tail = jnp.concatenate([tail[2 * n :], tail[: 2 * n]], axis=0)
                back = jnp.concatenate([back[:base], tail], axis=0)
                sig = jax.nn.sigmoid(gate)
                hidden = (gate * sig * up).astype(BF)
                delta = (back * up * sig * (1.0 + gate * (1.0 - sig))).astype(BF)
                hid = lax.dot_general(hidden, pi_ref[:, span], contract, preferred_element_type=F32)
                dlt = lax.dot_general(delta, po_ref[:, span], contract, preferred_element_type=F32)
                inner = hid if inner is None else inner + hid
                outer_ = dlt if outer_ is None else outer_ + dlt
            acc = jnp.concatenate([inner, outer_], axis=1)
            for i in range(NX):
                over = acc[base + 8 * i : base + 8 * i + 8]
                for a in range(n):
                    lo = i * main + a * MAIN
                    block = jnp.concatenate([acc[lo : lo + MAIN], over], axis=0).astype(BF)
                    done[a, i, k] = block
                    to = out_ref.at[spots_ref[i] if n_in > 1 else i, spots_ref[NX + a], k]
                    home.append(pltpu.make_async_copy(done.at[a, i, k], to, out_sem.at[a, i, k]))
                    home[-1].start()
        for c in home:
            c.wait()

    vmem, hbm = pl.BlockSpec(memory_space=pltpu.VMEM), pl.BlockSpec(memory_space=pltpu.HBM)
    return pl.pallas_call(
        kernel,
        name="expert",
        out_shape=[pltpu.HBM((NX, NZ, NC, part, 2 * r), BF), MARK],
        in_specs=[pl.BlockSpec(memory_space=pltpu.SMEM)]
        + [vmem] * n_in
        + [hbm] * 3
        + [vmem] * 5
        + [hbm] * len(extra)
        + [vmem] * len(after),
        out_specs=[hbm, vmem],
        input_output_aliases={1 + n_in + n_w + 2: 0} if extra else {},
        scratch_shapes=[
            pltpu.VMEM((chunks, d, chunk), BF),
            pltpu.VMEM((chunks, d, chunk), BF),
            pltpu.VMEM((chunks, d, chunk), BF),
            pltpu.VMEM((NC, m, d), BF),
            pltpu.VMEM((NC, m, d), BF),
            pltpu.VMEM((n, NX, NC, part, 2 * r), BF),
            pltpu.SemaphoreType.DMA((chunks, 3)),
            pltpu.SemaphoreType.DMA((n, NX, NC)),
        ],
        compiler_params=pltpu.CompilerParams(vmem_limit_bytes=VMEM),
    )(spots, *recv, *in_hbm(weights[:3]), *in_vmem(weights[3:]), proj_in, proj_out, *in_hbm(extra), *in_vmem(after))


def features(tokens, cotangent, proj_in, proj_out):
    t = tokens.shape[0]
    r = proj_in.shape[0]
    contract = (((1,), (1,)), ((), ()))

    def kernel(x_ref, c_ref, pi_ref, po_ref, out_ref):
        out_ref[:, 0:r] = lax.dot_general(x_ref[...], pi_ref[...], contract, preferred_element_type=F32).astype(BF)
        out_ref[:, r:] = lax.dot_general(c_ref[...], po_ref[...], contract, preferred_element_type=F32).astype(BF)

    return pl.pallas_call(
        kernel,
        name="features",
        out_shape=pltpu.VMEM((t, 2 * r), BF),
        compiler_params=pltpu.CompilerParams(vmem_limit_bytes=VMEM),
    )(tokens, cotangent, proj_in, proj_out)


def outer(ids, back, place, routes_t, weight_t, example, table, into=None):
    r = table.shape[1] // 2
    part = MAIN + 8
    k = NJ * part
    half = r // 2

    def kernel(ids_ref, routes_ref, weight_ref, ex_ref, table_ref, *refs):
        back_ref, refs = refs[0], refs[1:]
        if into is None:
            out_ref = refs[0]
        else:
            final_ref, out_ref, sem = refs[1:]
        routes = routes_ref[...].astype(F32)
        weight = weight_ref[...]
        example = ex_ref[...].astype(F32)
        lane = lax.broadcasted_iota(I32, (1, 2 * r), 1)
        col = lax.broadcasted_iota(I32, (k, NJ * 2 * r), 1) // (2 * r)
        row = lax.broadcasted_iota(I32, (k, NJ * 2 * r), 0) // part
        own = col == row
        pr = lax.broadcasted_iota(I32, (part, 1), 0)
        copies = []
        for p, shard in enumerate(place):
            eid = [ids_ref[p * NJ + j] for j in range(NJ)]
            keys = expert_keys(routes, [e.astype(F32) for e in eid])
            q = pr - MAIN - shard * SPARE
            slots = jnp.where(pr < MAIN, pr, jnp.where((q >= 0) & (q < SPARE), MAIN + q, -9)).astype(F32)
            hot, scale, held, second = [], [], [], []
            for j in range(NJ):
                h = jnp.where(keys[j : j + 1] == slots, 1.0, 0.0)
                we = jnp.sum(jnp.where(routes == eid[j].astype(F32), weight, 0.0), axis=0, keepdims=True)
                hot.append(h)
                scale.append(jnp.sum(h * we, axis=1, keepdims=True))
                held.append(jnp.sum(h, axis=1, keepdims=True))
                second.append(jnp.sum(h * example, axis=1, keepdims=True))
            hot = jnp.concatenate(hot, axis=0).astype(BF)
            scale = jnp.concatenate(scale, axis=0)
            held = jnp.concatenate(held, axis=0)
            second = jnp.concatenate(second, axis=0)
            mem = jnp.where(lane < r, held - second, second)
            sel = jnp.dot(hot, table_ref[...], preferred_element_type=F32) * scale
            at = ids_ref[len(place) * NJ + p]
            got = [back_ref[j // NC * NZ + at, j % NC].astype(F32) for j in range(NJ)]
            got = jnp.concatenate(got, axis=0)
            twice = lambda v: jnp.concatenate([v, v], axis=1)
            im = twice(sel[:, 0:r]) * mem
            om = twice(sel[:, r:])
            inner = twice(got[:, 0:r]) * mem
            outh = twice(got[:, r:])
            for g, (left, right) in enumerate(((im, outh), (inner, om))):
                wide = jnp.concatenate([right] * NJ, axis=1)
                wide = jnp.where(own, wide, 0.0).astype(BF)
                res = lax.dot_general(
                    left.astype(BF), wide, (((0,), (0,)), ((), ())), preferred_element_type=F32
                )
                for j in range(NJ):
                    for s in range(EX_DEV):
                        even = res[s * r : s * r + half, j * 2 * r : (j + 1) * 2 * r]
                        odd = res[s * r + half : (s + 1) * r, j * 2 * r : (j + 1) * 2 * r]
                        block = jnp.where(lane < r, even, odd).astype(BF)
                        if into is None:
                            out_ref[s, eid[j], g] = block
                        else:
                            out_ref[p, s, j, g] = block
            if into is not None:
                for s in range(EX_DEV):
                    for j in range(NJ):
                        to, i = final_ref.at[s, eid[j]], (p * EX_DEV + s) * NJ + j
                        copies.append(pltpu.make_async_copy(out_ref.at[p, s, j], to, sem.at[i]))
                        copies[-1].start()
        for c in copies:
            c.wait()

    vmem = pl.BlockSpec(memory_space=pltpu.VMEM)
    extra, out_specs, scratch, alias = [], vmem, [], {}
    if into is not None:
        extra, out_specs = [into], pl.BlockSpec(memory_space=pl.ANY)
        scratch = [
            pltpu.VMEM((len(place), EX_DEV, NJ, 2, half, 2 * r), BF),
            pltpu.SemaphoreType.DMA((len(place) * EX_DEV * NJ,)),
        ]
        alias = {6: 0}
    return pl.pallas_call(
        kernel,
        name="outer",
        out_shape=jax.ShapeDtypeStruct((EX_DEV, NZ * NJ, 2, half, 2 * r), BF),
        in_specs=[pl.BlockSpec(memory_space=pltpu.SMEM)]
        + [vmem] * 5
        + [pl.BlockSpec(memory_space=pl.ANY)] * len(extra),
        out_specs=out_specs,
        scratch_shapes=scratch,
        input_output_aliases=alias,
        compiler_params=pltpu.CompilerParams(vmem_limit_bytes=VMEM),
    )(ids, routes_t, weight_t, example, table, back, *extra)


def ordered(arrays, after):
    whole, vmem = pl.BlockSpec(memory_space=pltpu.HBM), pl.BlockSpec(memory_space=pltpu.VMEM)

    def kernel(*refs):
        refs[-1][...] = jnp.zeros_like(refs[-1])

    return pl.pallas_call(
        kernel,
        name="ordered",
        out_shape=[pltpu.HBM(a.shape, a.dtype) for a in arrays] + [MARK],
        in_specs=[whole] * len(arrays) + [vmem] * len(after),
        out_specs=[whole] * len(arrays) + [vmem],
        input_output_aliases={i: i for i in range(len(arrays))},
    )(*in_hbm(arrays), *in_vmem(after))


def pause(after):
    vmem = pl.BlockSpec(memory_space=pltpu.VMEM)

    def kernel(*refs):
        refs[-1][...] = jnp.zeros_like(refs[-1])

    return pl.pallas_call(
        kernel,
        name="pause",
        cost_estimate=LONG,
        out_shape=MARK,
        in_specs=[vmem] * len(after),
        out_specs=vmem,
    )(*in_vmem(after))


def along_z(a, k):
    return lax.ppermute(a, "z", [(i, (i + k) % NZ) for i in range(NZ)])


def along_x(a, k):
    return a if k == 0 else lax.ppermute(a, "x", [(i, (i + k) % NX) for i in range(NX)])


def partner(a):
    return lax.ppermute(a, "c", [(0, 1), (1, 0)])


def shards(
    tokens, cotangent, routes, route_weight, example_ids, w_gate, w_up, w_down, proj_model, proj_hidden
):
    tok_dev, d = tokens.shape
    r = proj_model.shape[0]
    x, z, c = (lax.axis_index(axis) for axis in ("x", "z", "c"))
    plane = lambda zz: jnp.stack(
        [(x + k) % NX * (NZ * NC) + zz * NC + (c ^ other) for k in STEPS_X for other in range(NC)]
    )
    here = jnp.concatenate([plane(z), jnp.stack([(x + k) % NX for k in STEPS_X])])

    routes_t = routes.T
    weight_t = route_weight.T
    own = assemble(tokens, cotangent, routes_t)

    order = lambda p: jnp.concatenate([p[0::2], p[1::2]], axis=0)
    proj_in, proj_out = order(proj_hidden), proj_hidden
    weights = [w_gate[0], w_up[0], w_down[0].T]
    weights = weights + [partner(w) for w in weights]
    table = features(tokens, cotangent, order(proj_model), proj_model)
    sources = [(x - k) % NX for k in STEPS_X]

    recvs, marks, back = [], [], None
    places = [[0], [-1, 1], [-2, 2], [-3, 3], [4]]

    def run_expert(i, into, after):
        spots = jnp.stack(sources + [(z + k) % NZ for k in places[i]])
        return expert(spots, recvs[i], len(places[i]), weights, proj_in, proj_out, into, after)

    for i, dist in enumerate(places):
        refs = [own]
        if i == 0:
            ahead, gap = [along_z(own, 1), along_z(own, -1)], [pause([])]
        elif i < 4:
            *refs, mark = ordered(ahead, [table, mark] if i == 1 else [mark, marks[i - 2]])
            gap = [pause([mark])]
            ahead = [along_z(refs[0], 1), along_z(refs[1], -1)] if i < 3 else [along_z(refs[0], 1)]
        else:
            refs, gap = ahead, []
        joined = i in JOINED
        *sent, mark = dispatch(refs, here, tok_dev, joined, gap + (marks[i - 2 : i - 1] if i >= 2 else []))
        if joined:
            recvs.append([lax.all_to_all(sent[0], "x", split_axis=0, concat_axis=0, tiled=True)])
        else:
            recvs.append([along_x(a, k) for a, k in zip(sent, STEPS_X)])
        if i:
            if i == 4:
                first, back = back, None
            back, done = run_expert(i - 1, back, [mark if i < 4 else pause([mark])])
            marks.append(done)

    back, _ = run_expert(4, back, [])

    def home(a):
        a = a.reshape((NX * NZ,) + a.shape[2:])
        return lax.all_to_all(a, ("x", "z"), split_axis=0, concat_axis=0, tiled=True)

    j = jnp.arange(NJ, dtype=I32)
    fixed = lambda zz: (j // NC) * (NZ * NC) + zz * NC + (c ^ (j % NC))
    mine = (routes_t, weight_t, example_ids[None, :], table)
    out = None
    for a, steps in ((first, places[:3]), (back, places[3:])):
        near = [(k, shard) for dist in steps for shard, k in enumerate(dist)]
        planes = [(z - k) % NZ for k, _ in near]
        ids = jnp.concatenate([fixed(p) for p in planes] + [jnp.stack(planes)])
        out = outer(ids, home(a), [shard for _, shard in near], *mine, into=out)
    return out.reshape(EX_DEV, NZ * NJ, 2, r * r)


def solution(mesh):
    dp = mesh.shape["dp"]
    torus = Mesh(mesh.devices.reshape(dp, NX, NZ, NC), ("dp", "x", "z", "c"))
    part, ex = ("dp", "x", "z", "c"), ("x", "z", "c")
    placed = (
        P(part, None),
        P(part, None),
        P(part, None),
        P(part, None),
        P(part),
        P(ex, None, None),
        P(ex, None, None),
        P(ex, None, None),
        P(),
        P(),
    )
    return jax.shard_map(
        shards, mesh=torus, in_specs=placed, out_specs=P(part, None, None, None), check_vma=False
    )
```

```python
import jax
import jax.numpy as jnp
from jax import lax
from jax.experimental import pallas as pl
from jax.experimental.pallas import tpu as pltpu
from jax.sharding import Mesh
from jax.sharding import PartitionSpec as P

NX, NZ, NC = 4, 8, 2
NJ = NX * NC
STEPS_X = (0, 1, 3, 2)
JOINED = (0, 2)
CAP, MAIN = 18, 16
SPARE = CAP - MAIN
EX_DEV = 2
BF, F32, I32 = jnp.bfloat16, jnp.float32, jnp.int32
VMEM = 24 * 1024 * 1024
MARK = pltpu.VMEM((8, 128), F32)
LONG = pl.CostEstimate(flops=int(4e10), bytes_accessed=int(12e6), transcendentals=0)


def in_hbm(arrays):
    return [pltpu.with_memory_space_constraint(a, pltpu.HBM) for a in arrays]


def in_vmem(arrays):
    return [pltpu.with_memory_space_constraint(a, pltpu.VMEM) for a in arrays]


def block_rows(n):
    return 2 * n * MAIN + 8


def row_slots(n, shard, array):
    r = lax.broadcasted_iota(I32, (n * MAIN + 8, 1), 0)
    base = shard * MAIN
    spare = n * MAIN + array * SPARE * n + shard * SPARE
    slot = jnp.where((r >= base) & (r < base + MAIN), r - base, -9)
    return jnp.where((r >= spare) & (r < spare + SPARE), MAIN + r - spare, slot)


def expert_keys(routes, ids):
    masks = [jnp.max(jnp.where(routes == e, 1.0, 0.0), axis=0, keepdims=True) for e in ids]
    mask = jnp.concatenate(masks, axis=0)
    t = mask.shape[1]
    before = lax.broadcasted_iota(I32, (t, t), 0) < lax.broadcasted_iota(I32, (t, t), 1)
    tri = jnp.where(before, 1.0, 0.0).astype(BF)
    rank = jnp.dot(mask.astype(BF), tri, preferred_element_type=F32)
    return jnp.where(mask > 0, rank, -1.0)


def assemble(tokens, cotangent, routes):
    t, d = tokens.shape

    parts = 4
    size = 2 * t // parts

    def kernel(x_ref, c_ref, routes_ref, out_ref, held, sem):
        def rows(i):
            return pl.ds(i * size, size)

        def copy_in(i):
            ref, at = (x_ref, i) if i < parts // 2 else (c_ref, i - parts // 2)
            return pltpu.make_async_copy(ref.at[rows(at)], held.at[rows(i)], sem.at[0, i])

        def copy_out(i):
            return pltpu.make_async_copy(held.at[rows(i)], out_ref.at[rows(i)], sem.at[1, i])

        for i in range(parts):
            copy_in(i).start()
        near = routes_ref[...].astype(F32)
        near = jnp.concatenate([near, jnp.zeros_like(near)], axis=0).astype(BF)
        held[2 * t :, :] = jnp.zeros((16, d), BF)
        held[2 * t :, 0:t] = near
        last = pl.ds(2 * t, 16)
        tail = pltpu.make_async_copy(held.at[last], out_ref.at[last], sem.at[0, parts])
        tail.start()
        for i in range(parts):
            copy_in(i).wait()
            copy_out(i).start()
        for i in range(parts):
            copy_out(i).wait()
        tail.wait()

    hbm = pl.BlockSpec(memory_space=pltpu.HBM)
    return pl.pallas_call(
        kernel,
        name="assemble",
        out_shape=pltpu.HBM((2 * t + 16, d), BF),
        in_specs=[hbm, hbm, pl.BlockSpec(memory_space=pltpu.VMEM)],
        out_specs=hbm,
        scratch_shapes=[pltpu.VMEM((2 * t + 16, d), BF), pltpu.SemaphoreType.DMA((2, parts + 1))],
    )(*in_hbm([tokens, cotangent]), routes)


def dispatch(shard_refs, ids, tok_dev, joined, after=()):
    n = len(shard_refs)
    rows = block_rows(n)
    d = shard_refs[0].shape[1]
    chunks = 4
    cols = d // chunks
    both = 2 * tok_dev
    main = n * MAIN
    n_out, lead = (1, (NX,)) if joined else (NX, ())

    def kernel(ids_ref, *refs):
        ins, refs = refs[:n], refs[n + len(after) :]
        outs, mark_ref = refs[:n_out], refs[n_out]
        held, sent, hot_ref, near, in_sem, out_sem, near_sem = refs[n_out + 1 :]

        def span(q):
            return pl.ds(q * cols, cols)

        def copies_in(q):
            return [
                pltpu.make_async_copy(
                    ins[i].at[pl.ds(array * tok_dev, tok_dev), span(q)],
                    held.at[array, pl.ds(i * tok_dev, tok_dev), span(q)],
                    in_sem.at[i, q, array],
                )
                for i in range(n)
                for array in range(2)
            ]

        def copy_out(i, q):
            to = outs[0].at[ids_ref[NJ + i]] if joined else outs[i]
            src = sent.at[pl.ds(i * NC, NC), :, span(q)]
            return pltpu.make_async_copy(src, to.at[:, :, span(q)], out_sem.at[i, q])

        def copy_near(i):
            src = ins[i].at[pl.ds(both, 16), pl.ds(0, tok_dev)]
            return pltpu.make_async_copy(src, near.at[i], near_sem.at[i])

        for i in range(n):
            copy_near(i).start()
        for q in range(chunks):
            for c in copies_in(q):
                c.start()
        mark_ref[...] = jnp.zeros_like(mark_ref)
        eid = [ids_ref[j].astype(F32) for j in range(NJ)]
        for a in range(n):
            copy_near(a).wait()
            keys = expert_keys(near[a].astype(F32)[0:8], eid)
            for array in range(2):
                slots = row_slots(n, a, array).astype(F32)
                hot = [jnp.where(keys[j : j + 1] == slots, 1.0, 0.0) for j in range(NJ)]
                hot = jnp.concatenate(hot, axis=0).astype(BF)
                hot_ref[array, :, a * tok_dev : (a + 1) * tok_dev] = hot
        for q in range(chunks):
            for c in copies_in(q):
                c.wait()
            here = slice(q * cols, (q + 1) * cols)
            x, c = [jnp.dot(hot_ref[i], held[i, :, here], preferred_element_type=F32) for i in range(2)]
            for j in range(NJ):
                at = j * (main + 8)
                sent[j, 0:main, here] = x[at : at + main].astype(BF)
                sent[j, main : 2 * main, here] = c[at : at + main].astype(BF)
                at += main
                sent[j, 2 * main :, here] = (x[at : at + 8] + c[at : at + 8]).astype(BF)
            for i in range(NX):
                copy_out(i, q).start()
        for q in range(chunks):
            for i in range(NX):
                copy_out(i, q).wait()

    vmem, hbm = pl.BlockSpec(memory_space=pltpu.VMEM), pl.BlockSpec(memory_space=pltpu.HBM)
    return pl.pallas_call(
        kernel,
        name="dispatch",
        out_shape=[pltpu.HBM(lead + (NC, rows, d), BF)] * n_out + [MARK],
        in_specs=[pl.BlockSpec(memory_space=pltpu.SMEM)] + [hbm] * n + [vmem] * len(after),
        out_specs=[hbm] * n_out + [vmem],
        scratch_shapes=[
            pltpu.VMEM((2, n * tok_dev, d), BF),
            pltpu.VMEM((NJ, rows, d), BF),
            pltpu.VMEM((2, NJ * (main + 8), n * tok_dev), BF),
            pltpu.VMEM((n, 16, tok_dev), BF),
            pltpu.SemaphoreType.DMA((n, chunks, 2)),
            pltpu.SemaphoreType.DMA((NX, chunks)),
            pltpu.SemaphoreType.DMA((n,)),
        ],
        compiler_params=pltpu.CompilerParams(vmem_limit_bytes=VMEM),
    )(ids, *in_hbm(shard_refs), *in_vmem(after))


def expert(spots, recv, n, weights, proj_in, proj_out, into, after=()):
    rows, d = recv[0].shape[-2:]
    n_in = len(recv)
    ff = weights[0].shape[-1]
    r = proj_in.shape[0]
    chunk = 256
    chunks = ff // chunk
    n_w = len(weights)
    main = n * MAIN
    base = NX * main
    m = base + NX * 8
    part = MAIN + 8
    contract = (((1,), (1,)), ((), ()))

    extra = [] if into is None else [into]

    def kernel(spots_ref, *refs):
        x_refs = refs[:n_in] if n_in > 1 else [refs[0].at[i] for i in range(NX)]
        w_refs = refs[n_in : n_in + n_w]
        pi_ref, po_ref = refs[n_in + n_w : n_in + n_w + 2]
        refs = refs[n_in + n_w + 2 + len(extra) + len(after) :]
        out_ref, mark_ref, wg, wu, wd, xs, cs, done, sem, out_sem = refs
        mark_ref[...] = jnp.zeros_like(mark_ref)
        gate_w, up_w, down_w = w_refs[:3]

        def copies(f):
            span = pl.ds(f * chunk, chunk)
            return (
                pltpu.make_async_copy(gate_w.at[:, span], wg.at[f], sem.at[f, 0]),
                pltpu.make_async_copy(up_w.at[:, span], wu.at[f], sem.at[f, 1]),
                pltpu.make_async_copy(down_w.at[:, span], wd.at[f], sem.at[f, 2]),
            )

        for f in range(chunks):
            for c in copies(f):
                c.start()
        for i in reversed(range(NX)):
            for k in range(NC):
                xs[k, i * main : (i + 1) * main, :] = x_refs[i][k, 0:main, :]
                cs[k, i * main : (i + 1) * main, :] = x_refs[i][k, main : 2 * main, :]
        for k in range(NC):
            spare = [x_refs[i][k, 2 * main : 2 * main + 8, :].astype(F32) for i in range(NX)]
            spare = jnp.concatenate(spare, axis=0).astype(BF)
            xs[k, base:, :] = spare
            cs[k, base:, :] = spare
        home = []
        for k in reversed(range(NC)):
            inner, outer_ = None, None
            for f in range(1 if k else chunks):
                span = slice(0, ff) if k else slice(f * chunk, (f + 1) * chunk)
                if k:
                    gate_c, up_c, down_c = w_refs[3][:, span], w_refs[4][:, span], w_refs[5][:, span]
                else:
                    for c in copies(f):
                        c.wait()
                    gate_c, up_c, down_c = wg[f], wu[f], wd[f]
                x = xs[k]
                gate = jnp.dot(x, gate_c, preferred_element_type=F32)
                up = jnp.dot(x, up_c, preferred_element_type=F32)
                back = jnp.dot(cs[k], down_c, preferred_element_type=F32)
                tail = back[base:]
                tail = jnp.concatenate([tail[2 * n :], tail[: 2 * n]], axis=0)
                back = jnp.concatenate([back[:base], tail], axis=0)
                sig = jax.nn.sigmoid(gate)
                hidden = (gate * sig * up).astype(BF)
                delta = (back * up * sig * (1.0 + gate * (1.0 - sig))).astype(BF)
                hid = lax.dot_general(hidden, pi_ref[:, span], contract, preferred_element_type=F32)
                dlt = lax.dot_general(delta, po_ref[:, span], contract, preferred_element_type=F32)
                inner = hid if inner is None else inner + hid
                outer_ = dlt if outer_ is None else outer_ + dlt
            acc = jnp.concatenate([inner, outer_], axis=1)
            for i in range(NX):
                over = acc[base + 8 * i : base + 8 * i + 8]
                for a in range(n):
                    lo = i * main + a * MAIN
                    block = jnp.concatenate([acc[lo : lo + MAIN], over], axis=0).astype(BF)
                    done[a, i, k] = block
                    to = out_ref.at[spots_ref[i] if n_in > 1 else i, spots_ref[NX + a], k]
                    home.append(pltpu.make_async_copy(done.at[a, i, k], to, out_sem.at[a, i, k]))
                    home[-1].start()
        for c in home:
            c.wait()

    vmem, hbm = pl.BlockSpec(memory_space=pltpu.VMEM), pl.BlockSpec(memory_space=pltpu.HBM)
    return pl.pallas_call(
        kernel,
        name="expert",
        out_shape=[pltpu.HBM((NX, NZ, NC, part, 2 * r), BF), MARK],
        in_specs=[pl.BlockSpec(memory_space=pltpu.SMEM)]
        + [vmem] * n_in
        + [hbm] * 3
        + [vmem] * 5
        + [hbm] * len(extra)
        + [vmem] * len(after),
        out_specs=[hbm, vmem],
        input_output_aliases={1 + n_in + n_w + 2: 0} if extra else {},
        scratch_shapes=[
            pltpu.VMEM((chunks, d, chunk), BF),
            pltpu.VMEM((chunks, d, chunk), BF),
            pltpu.VMEM((chunks, d, chunk), BF),
            pltpu.VMEM((NC, m, d), BF),
            pltpu.VMEM((NC, m, d), BF),
            pltpu.VMEM((n, NX, NC, part, 2 * r), BF),
            pltpu.SemaphoreType.DMA((chunks, 3)),
            pltpu.SemaphoreType.DMA((n, NX, NC)),
        ],
        compiler_params=pltpu.CompilerParams(vmem_limit_bytes=VMEM),
    )(spots, *recv, *in_hbm(weights[:3]), *in_vmem(weights[3:]), proj_in, proj_out, *in_hbm(extra), *in_vmem(after))


def features(tokens, cotangent, proj_in, proj_out):
    t = tokens.shape[0]
    r = proj_in.shape[0]
    contract = (((1,), (1,)), ((), ()))

    def kernel(x_ref, c_ref, pi_ref, po_ref, out_ref):
        out_ref[:, 0:r] = lax.dot_general(x_ref[...], pi_ref[...], contract, preferred_element_type=F32).astype(BF)
        out_ref[:, r:] = lax.dot_general(c_ref[...], po_ref[...], contract, preferred_element_type=F32).astype(BF)

    return pl.pallas_call(
        kernel,
        name="features",
        out_shape=pltpu.VMEM((t, 2 * r), BF),
        compiler_params=pltpu.CompilerParams(vmem_limit_bytes=VMEM),
    )(tokens, cotangent, proj_in, proj_out)


def outer(ids, back, place, routes_t, weight_t, example, table, into=None):
    r = table.shape[1] // 2
    part = MAIN + 8
    k = NJ * part
    half = r // 2

    def kernel(ids_ref, routes_ref, weight_ref, ex_ref, table_ref, *refs):
        back_ref, refs = refs[0], refs[1:]
        if into is None:
            out_ref = refs[0]
        else:
            final_ref, out_ref, sem = refs[1:]
        routes = routes_ref[...].astype(F32)
        weight = weight_ref[...]
        example = ex_ref[...].astype(F32)
        lane = lax.broadcasted_iota(I32, (1, 2 * r), 1)
        col = lax.broadcasted_iota(I32, (k, NJ * 2 * r), 1) // (2 * r)
        row = lax.broadcasted_iota(I32, (k, NJ * 2 * r), 0) // part
        own = col == row
        pr = lax.broadcasted_iota(I32, (part, 1), 0)
        copies = []
        for p, shard in enumerate(place):
            eid = [ids_ref[p * NJ + j] for j in range(NJ)]
            keys = expert_keys(routes, [e.astype(F32) for e in eid])
            q = pr - MAIN - shard * SPARE
            slots = jnp.where(pr < MAIN, pr, jnp.where((q >= 0) & (q < SPARE), MAIN + q, -9)).astype(F32)
            hot, scale, held, second = [], [], [], []
            for j in range(NJ):
                h = jnp.where(keys[j : j + 1] == slots, 1.0, 0.0)
                we = jnp.sum(jnp.where(routes == eid[j].astype(F32), weight, 0.0), axis=0, keepdims=True)
                hot.append(h)
                scale.append(jnp.sum(h * we, axis=1, keepdims=True))
                held.append(jnp.sum(h, axis=1, keepdims=True))
                second.append(jnp.sum(h * example, axis=1, keepdims=True))
            hot = jnp.concatenate(hot, axis=0).astype(BF)
            scale = jnp.concatenate(scale, axis=0)
            held = jnp.concatenate(held, axis=0)
            second = jnp.concatenate(second, axis=0)
            mem = jnp.where(lane < r, held - second, second)
            sel = jnp.dot(hot, table_ref[...], preferred_element_type=F32) * scale
            at = ids_ref[len(place) * NJ + p]
            got = [back_ref[j // NC * NZ + at, j % NC].astype(F32) for j in range(NJ)]
            got = jnp.concatenate(got, axis=0)
            twice = lambda v: jnp.concatenate([v, v], axis=1)
            im = twice(sel[:, 0:r]) * mem
            om = twice(sel[:, r:])
            inner = twice(got[:, 0:r]) * mem
            outh = twice(got[:, r:])
            for g, (left, right) in enumerate(((im, outh), (inner, om))):
                wide = jnp.concatenate([right] * NJ, axis=1)
                wide = jnp.where(own, wide, 0.0).astype(BF)
                res = lax.dot_general(
                    left.astype(BF), wide, (((0,), (0,)), ((), ())), preferred_element_type=F32
                )
                for j in range(NJ):
                    for s in range(EX_DEV):
                        even = res[s * r : s * r + half, j * 2 * r : (j + 1) * 2 * r]
                        odd = res[s * r + half : (s + 1) * r, j * 2 * r : (j + 1) * 2 * r]
                        block = jnp.where(lane < r, even, odd).astype(BF)
                        if into is None:
                            out_ref[s, eid[j], g] = block
                        else:
                            out_ref[p, s, j, g] = block
            if into is not None:
                for s in range(EX_DEV):
                    for j in range(NJ):
                        to, i = final_ref.at[s, eid[j]], (p * EX_DEV + s) * NJ + j
                        copies.append(pltpu.make_async_copy(out_ref.at[p, s, j], to, sem.at[i]))
                        copies[-1].start()
        for c in copies:
            c.wait()

    vmem = pl.BlockSpec(memory_space=pltpu.VMEM)
    extra, out_specs, scratch, alias = [], vmem, [], {}
    if into is not None:
        extra, out_specs = [into], pl.BlockSpec(memory_space=pl.ANY)
        scratch = [
            pltpu.VMEM((len(place), EX_DEV, NJ, 2, half, 2 * r), BF),
            pltpu.SemaphoreType.DMA((len(place) * EX_DEV * NJ,)),
        ]
        alias = {6: 0}
    return pl.pallas_call(
        kernel,
        name="outer",
        out_shape=jax.ShapeDtypeStruct((EX_DEV, NZ * NJ, 2, half, 2 * r), BF),
        in_specs=[pl.BlockSpec(memory_space=pltpu.SMEM)]
        + [vmem] * 5
        + [pl.BlockSpec(memory_space=pl.ANY)] * len(extra),
        out_specs=out_specs,
        scratch_shapes=scratch,
        input_output_aliases=alias,
        compiler_params=pltpu.CompilerParams(vmem_limit_bytes=VMEM),
    )(ids, routes_t, weight_t, example, table, back, *extra)


def ordered(arrays, after):
    whole, vmem = pl.BlockSpec(memory_space=pltpu.HBM), pl.BlockSpec(memory_space=pltpu.VMEM)

    def kernel(*refs):
        refs[-1][...] = jnp.zeros_like(refs[-1])

    return pl.pallas_call(
        kernel,
        name="ordered",
        out_shape=[pltpu.HBM(a.shape, a.dtype) for a in arrays] + [MARK],
        in_specs=[whole] * len(arrays) + [vmem] * len(after),
        out_specs=[whole] * len(arrays) + [vmem],
        input_output_aliases={i: i for i in range(len(arrays))},
    )(*in_hbm(arrays), *in_vmem(after))


def pause(after):
    vmem = pl.BlockSpec(memory_space=pltpu.VMEM)

    def kernel(*refs):
        refs[-1][...] = jnp.zeros_like(refs[-1])

    return pl.pallas_call(
        kernel,
        name="pause",
        cost_estimate=LONG,
        out_shape=MARK,
        in_specs=[vmem] * len(after),
        out_specs=vmem,
    )(*in_vmem(after))


def along_z(a, k):
    return lax.ppermute(a, "z", [(i, (i + k) % NZ) for i in range(NZ)])


def along_x(a, k):
    return a if k == 0 else lax.ppermute(a, "x", [(i, (i + k) % NX) for i in range(NX)])


def partner(a):
    return lax.ppermute(a, "c", [(0, 1), (1, 0)])


def shards(
    tokens, cotangent, routes, route_weight, example_ids, w_gate, w_up, w_down, proj_model, proj_hidden
):
    tok_dev, d = tokens.shape
    r = proj_model.shape[0]
    x, z, c = (lax.axis_index(axis) for axis in ("x", "z", "c"))
    plane = lambda zz: jnp.stack(
        [(x + k) % NX * (NZ * NC) + zz * NC + (c ^ other) for k in STEPS_X for other in range(NC)]
    )
    here = jnp.concatenate([plane(z), jnp.stack([(x + k) % NX for k in STEPS_X])])

    routes_t = routes.T
    weight_t = route_weight.T
    own = assemble(tokens, cotangent, routes_t)

    order = lambda p: jnp.concatenate([p[0::2], p[1::2]], axis=0)
    proj_in, proj_out = order(proj_hidden), proj_hidden
    weights = [w_gate[0], w_up[0], w_down[0].T]
    weights = weights + [partner(w) for w in weights]
    table = features(tokens, cotangent, order(proj_model), proj_model)
    sources = [(x - k) % NX for k in STEPS_X]

    recvs, marks, back = [], [], None
    places = [[0], [-1, 1], [-2, 2], [-3, 3], [4]]

    def run_expert(i, into, after):
        spots = jnp.stack(sources + [(z + k) % NZ for k in places[i]])
        return expert(spots, recvs[i], len(places[i]), weights, proj_in, proj_out, into, after)

    for i, dist in enumerate(places):
        refs = [own]
        if i == 0:
            ahead, gap = [along_z(own, 1), along_z(own, -1)], [pause([])]
        elif i < 4:
            *refs, mark = ordered(ahead, [table, mark] if i == 1 else [mark, marks[i - 2]])
            gap = [pause([mark])]
            ahead = [along_z(refs[0], 1), along_z(refs[1], -1)] if i < 3 else [along_z(refs[0], 1)]
        else:
            refs, gap = ahead, []
        joined = i in JOINED
        *sent, mark = dispatch(refs, here, tok_dev, joined, gap + (marks[i - 2 : i - 1] if i >= 2 else []))
        if joined:
            recvs.append([lax.all_to_all(sent[0], "x", split_axis=0, concat_axis=0, tiled=True)])
        else:
            recvs.append([along_x(a, k) for a, k in zip(sent, STEPS_X)])
        if i:
            if i == 4:
                first, back = back, None
            back, done = run_expert(i - 1, back, [mark if i < 4 else pause([mark])])
            marks.append(done)

    back, _ = run_expert(4, back, [])

    def home(a):
        a = a.reshape((NX * NZ,) + a.shape[2:])
        return lax.all_to_all(a, ("x", "z"), split_axis=0, concat_axis=0, tiled=True)

    j = jnp.arange(NJ, dtype=I32)
    fixed = lambda zz: (j // NC) * (NZ * NC) + zz * NC + (c ^ (j % NC))
    mine = (routes_t, weight_t, example_ids[None, :], table)
    out = None
    for a, steps in ((first, places[:3]), (back, places[3:])):
        near = [(k, shard) for dist in steps for shard, k in enumerate(dist)]
        planes = [(z - k) % NZ for k, _ in near]
        ids = jnp.concatenate([fixed(p) for p in planes] + [jnp.stack(planes)])
        out = outer(ids, home(a), [shard for _, shard in near], *mine, into=out)
    return out.reshape(EX_DEV, NZ * NJ, 2, r * r)


def solution(mesh):
    dp = mesh.shape["dp"]
    torus = Mesh(mesh.devices.reshape(dp, NX, NZ, NC), ("dp", "x", "z", "c"))
    part, ex = ("dp", "x", "z", "c"), ("x", "z", "c")
    placed = (
        P(part, None),
        P(part, None),
        P(part, None),
        P(part, None),
        P(part),
        P(ex, None, None),
        P(ex, None, None),
        P(ex, None, None),
        P(),
        P(),
    )
    return jax.shard_map(
        shards, mesh=torus, in_specs=placed, out_specs=P(part, None, None, None), check_vma=False
    )
```
